256 devices in a mesh: frames: 64 (over x, y, z_lo, core), chan: 4 (over z_hi).
Axes of the slice: x: 4, y: 4, z: 8 (z_hi: 4, z_lo: 2; z = z_hi * 2 + z_lo), core: 2. Of those that a mesh axis runs over, the one named last changes fastest.
Arguments:
- inputs: bfloat16 [128, 256, 16, 128], P('frames', 'chan'), may hold values from -6 to 6
- saved: bfloat16 [128, 256, 16, 128], P('frames', 'chan'), may hold values from -6 to 6
- cotangent: bfloat16 [64, 256, 512], P('frames', 'chan'), may hold values from -24 to 24
- spatial_w: bfloat16 [3, 3, 256, 256], P(None, None, 'chan'), may hold values from -0.125 to 0.125
- temporal_w: bfloat16 [3, 256, 256], replicated, may hold values from -0.21875 to 0.21875
Outputs:
- input_grad: bfloat16 [128, 256, 16, 128], P('frames', 'chan')
- spatial_grad: float32 [3, 3, 256, 256], P(None, None, 'chan')
- temporal_grad: float32 [3, 256, 256], P(None, 'chan')
The draws below stay inside these ranges and needn't reach their ends.
All inputs are finite; a program needn't handle non-finite values.
Results may differ from the reference program's by a relative error of at most 0.0049.
Values may be sent and summed in bfloat16 or wider, within the bound.
A program may use at most 64 MiB of HBM per device.

```python
import math
import jax
import jax.numpy as jnp

C = 256
W = 128
H = 16
FRAMES = 128
POOLED = 512


def levels(key, dims, pieces, low, high):
    gain = 1.0
    for position, shards_of in pieces:
        draws = jax.random.uniform(jax.random.fold_in(jax.random.fold_in(key, 6), position), (shards_of,), jnp.float32, low / len(pieces), high / len(pieces))
        gain = gain * jnp.repeat(jnp.exp(draws), dims[position] // shards_of).reshape((-1,) + (1,) * (len(dims) - 1 - position))
    return gain


def noise(rng, shape, width, most, split=(), dtype=jnp.bfloat16):
    values = width * jax.random.normal(rng, shape, jnp.float32)
    if split:
        values = values * levels(rng, shape, split, -0.22, 0.18)
    return jnp.clip(values, -most, most).astype(dtype)


def setup_inputs(seed: int = 0) -> dict:
    key_list = jax.random.split(jax.random.key(seed), 6)
    return {
        "inputs": noise(key_list[0], (FRAMES, C, H, W), 1.0, 6.0, ((0, 64), (1, 4))),
        "saved": noise(key_list[1], (FRAMES, C, H, W), 1.0, 6.0, ((0, 64), (1, 4))),
        "cotangent": noise(key_list[2], (FRAMES // 2, C, POOLED), 4.0, 24.0, ((0, 64), (1, 4))),
        "spatial_w": noise(key_list[3], (3, 3, C, C), (9 * C) ** -0.5, 0.125, ((2, 4),)),
        "temporal_w": noise(key_list[4], (3, C, C), (3 * C) ** -0.5, 0.21875),
    }


def reference(inputs, saved, cotangent, spatial_w, temporal_w):
    wide = jnp.float32
    scale = 1.0 / math.sqrt(FRAMES * H * W)
    half = cotangent.reshape(FRAMES // 2, C, H // 2, W // 2).astype(wide) * 0.125
    upsampled = jnp.repeat(jnp.repeat(jnp.repeat(half, 2, axis=0), 2, axis=2), 2, axis=3).astype(jnp.bfloat16)
    frame_pad = ((1, 1), (0, 0), (0, 0), (0, 0))
    up_pad = jnp.pad(upsampled.astype(wide), frame_pad)
    saved_pad = jnp.pad(saved.astype(wide), frame_pad)
    wide_t = temporal_w.astype(wide)
    grad_sum = jnp.zeros((FRAMES, C, H, W), wide)
    for tap in range(3):
        grad_sum = grad_sum + jnp.einsum('fohw,io->fihw', up_pad[2 - tap:2 - tap + FRAMES], wide_t[tap])
    saved_grad = grad_sum.astype(jnp.bfloat16)
    temporal_grad = jnp.stack([jnp.einsum('fihw,fohw->io', saved_pad[tap:tap + FRAMES], up_pad[1:FRAMES + 1]) for tap in range(3)]) * scale
    space_pad = ((0, 0), (0, 0), (1, 1), (1, 1))
    grad_wide = saved_grad.astype(wide)
    grad_pad = jnp.pad(grad_wide, space_pad)
    input_pad = jnp.pad(inputs.astype(wide), space_pad)
    wide_s = spatial_w.astype(wide)
    input_sum = jnp.zeros((FRAMES, C, H, W), wide)
    kernel_rows = []
    for tap_row in range(3):
        kernel_cols = []
        for tap_col in range(3):
            window = grad_pad[:, :, 2 - tap_row:2 - tap_row + H, 2 - tap_col:2 - tap_col + W]
            input_sum = input_sum + jnp.einsum('fohw,io->fihw', window, wide_s[tap_row, tap_col])
            shifted = input_pad[:, :, tap_row:tap_row + H, tap_col:tap_col + W]
            kernel_cols.append(jnp.einsum('fihw,fohw->io', shifted, grad_wide))
        kernel_rows.append(jnp.stack(kernel_cols))
    spatial_grad = jnp.stack(kernel_rows) * scale
    return (input_sum.astype(jnp.bfloat16), spatial_grad, temporal_grad)
```

```python
import math

import jax
import jax.numpy as jnp
from jax import lax
from jax.experimental import pallas as pl
from jax.experimental.pallas import tpu as pltpu
from jax.sharding import PartitionSpec as P

BF = jnp.bfloat16
F32 = jnp.float32
CHIPS = 32
UNITS = 24


def dot(a, b):
    return jnp.dot(a, b, preferred_element_type=F32)


def dot_nt(a, b):
    return lax.dot_general(a, b, (((1,), (1,)), ((), ())), preferred_element_type=F32)


def kernel(
    x_h, s_h, c_h, sw_h, tw_h,
    ig_h, gr_v,
    x_v, s_v, sw_v, tw_v, ring, halo, pool, q_v, sq_v, a_v, g_v, p_v, xe_v, z_v, out_v,
    partf, part, xch, half_v, rs_v,
    load_sem, ring_send, ring_recv, fwd_send, halo_recv,
    xch_send, xch_recv, rs_send, rs_recv, ag_send, ag_recv, sib_send, sib_recv, out_sem,
):
    p = lax.axis_index("frames")
    c = lax.axis_index("chan")
    core = lax.rem(p, 2)
    chip = lax.div(p, 2)
    zl = lax.rem(chip, 2)
    column = lax.div(chip, 2)
    z = 2 * c + zl

    def at_z(zz):
        zz = lax.rem(zz, 8)
        return (4 * column + 2 * lax.rem(zz, 2) + core, lax.div(zz, 2))

    up, down = at_z(z + 1), at_z(z + 7)
    sibling = (p + 1 - 2 * core, c)
    differ = jnp.where(zl == core, 0, 1)
    to_step = jnp.where(zl == core, 1 - 2 * core, jnp.where(core == 1, 3, -3))
    from_step = jnp.where(zl == core, jnp.where(core == 0, -3, 3), jnp.where(core == 1, -1, 1))
    to_frame, from_frame = p + to_step, p + from_step
    last = 4 * 16
    to_ok = jnp.logical_and(to_frame >= 0, to_frame < last)
    from_ok = jnp.logical_and(from_frame >= 0, from_frame < last)

    barrier = pltpu.get_barrier_semaphore()

    def greet(device):
        pl.semaphore_signal(barrier, inc=1, device_id=device, device_id_type=pl.DeviceIdType.MESH)

    greet(up)
    greet(down)
    greet(sibling)

    @pl.when(to_ok)
    def _():
        greet((to_frame, c))

    @pl.when(from_ok)
    def _():
        greet((from_frame, c))

    def greet_chip(j, carry):
        greet((2 * lax.rem(chip + j, CHIPS) + core, c))
        return carry

    lax.fori_loop(1, CHIPS, greet_chip, 0)

    loads = [
        pltpu.make_async_copy(c_h.at[0], ring.at[0, c], load_sem.at[0]),
        pltpu.make_async_copy(s_h, s_v, load_sem.at[1]),
        pltpu.make_async_copy(x_h, x_v, load_sem.at[2]),
        pltpu.make_async_copy(tw_h, tw_v, load_sem.at[3]),
        pltpu.make_async_copy(sw_h, sw_v, load_sem.at[4]),
    ]
    for load in loads:
        load.start()

    pl.semaphore_wait(
        barrier, 34 + jnp.where(to_ok, 1, 0) + jnp.where(from_ok, 1, 0)
    )

    def remote(src, dst, send, recv, device):
        return pltpu.make_async_remote_copy(
            src_ref=src, dst_ref=dst, send_sem=send, recv_sem=recv,
            device_id=device, device_id_type=pl.DeviceIdType.MESH,
        )

    sent = []

    def rows(half):
        return pl.ds(32 * half, 32)

    def ring_send_step(way, step, half):
        zz = z + (8 - step if way == 0 else step)
        quarter = lax.div(lax.rem(zz, 8), 2)
        if step == 0:
            src = c_h.at[0, rows(half)]
        else:
            src = ring.at[step % 2, quarter, rows(half)]
        copy = remote(
            src, ring.at[(step + 1) % 2, quarter, rows(half)],
            ring_send.at[way, step, half], ring_recv.at[way, step, half],
            up if way == 0 else down,
        )
        copy.start()
        sent.append(copy)

    def ring_wait_step(way, step, half):
        zz = z + (7 - step if way == 0 else 1 + step)
        quarter = lax.div(lax.rem(zz, 8), 2)
        dst = ring.at[(step + 1) % 2, quarter, rows(half)]
        remote(
            dst, dst, ring_send.at[way, step, half], ring_recv.at[way, step, half],
            down if way == 0 else up,
        ).wait_recv()
        return quarter

    def forward_own(src, quarter, index):
        copy = remote(src, halo.at[core, quarter], fwd_send.at[index], halo_recv.at[0], sibling)
        copy.start()
        sent.append(copy)

    def forward_other(quarter, index):
        copy = remote(
            ring.at[1, quarter], halo.at[1 - core, quarter],
            fwd_send.at[index], halo_recv.at[1], (to_frame, c),
        )

        @pl.when(to_ok)
        def _():
            copy.start()

        return copy

    for half in range(2):
        ring_send_step(0, 0, half)
        ring_send_step(1, 0, half)
    forward_own(c_h.at[0], c, 0)

    lane = lax.broadcasted_iota(jnp.int32, (128, 384), 1)
    column_of = lax.broadcasted_iota(jnp.int32, (128, 384), 0)
    first = 2 * (lane & 63) + (lane >> 7) - 1
    pairs = jnp.where(
        jnp.logical_or(column_of == first, column_of == first + 1), 1.0, 0.0
    ).astype(BF)
    low = lax.broadcasted_iota(jnp.int32, (64, 128), 1) < 64

    loads[1].wait()
    for f in range(2):
        pool[0, pl.ds(f * 1024, 1024), :] = dot(
            s_v[f].reshape(1024, 128), pairs[:, 128:256]
        )
        height = [pool[0, pl.ds(f * 1024 + h, 64, stride=16), :] for h in range(16)]
        for j in range(4):
            upper = height[4 * j] + height[4 * j + 1]
            lower = height[4 * j + 2] + height[4 * j + 3]
            sq_v[pl.ds(64 * f, 64), 128 * j : 128 * j + 128] = jnp.where(low, upper, lower).astype(BF)

    others = []

    def ring_step(step):
        for way in range(2):
            for half in range(2):
                if step == 3 and half != way:
                    continue
                quarter = ring_wait_step(way, step, half)
                if step < 2 or (step == 2 and half == way):
                    ring_send_step(way, step + 1, half)
            if step == 0 or step == 2:
                others.append(forward_other(quarter, 4 + step + way))
            elif step == 1:
                forward_own(ring.at[0, quarter], quarter, 1 + way)
        if step == 3:
            forward_own(ring.at[0, quarter], quarter, 3)

    ring_step(0)
    loads[2].wait()
    for f in range(2):
        sums = dot(x_v[f].reshape(1024, 128), pairs)
        for b in range(3):
            pool[1 + b, pl.ds(f * 1024, 1024), :] = sums[:, 128 * b : 128 * b + 128]
    ring_step(1)
    for f in range(2):
        for b in range(3):
            height = [pool[1 + b, pl.ds(f * 1024 + h, 64, stride=16), :] for h in range(16)]
            total = (
                [height[0]] + [height[h] + height[h + 1] for h in range(15)] + [height[15]]
            )
            for a in range(3):
                for j in range(4):
                    q_v[f, pl.ds((3 * a + b) * 64, 64), 128 * j : 128 * j + 128] = jnp.where(
                        low, total[4 * j + a], total[4 * j + a + 2]
                    ).astype(BF)
        if f == 0:
            ring_step(2)
    loads[0].wait()
    loads[3].wait()
    ring_step(3)

    own = ring[0].reshape(256, 512)
    a_v[...] = dot(tw_v[...].reshape(768, 256), own)
    t_own = dot_nt(sq_v[...], own)

    dst = halo.at[1 - core]
    pltpu.make_async_copy(dst, dst, halo_recv.at[0]).wait()

    @pl.when(from_ok)
    def _():
        dst = halo.at[core]
        pltpu.make_async_copy(dst, dst, halo_recv.at[1]).wait()

    @pl.when(jnp.logical_not(from_ok))
    def _():
        halo[core] = jnp.zeros((4, 64, 512), BF)

    before = halo[0].reshape(256, 512)
    after = halo[1].reshape(256, 512)
    middle = a_v[256:512]
    g_v[0] = ((a_v[0:256] + middle + dot(tw_v[2], before)) * 0.125).astype(BF)
    g_v[1] = ((dot(tw_v[0], after) + middle + a_v[512:768]) * 0.125).astype(BF)

    t_after = dot_nt(sq_v[64:128], after)
    t_before = dot_nt(sq_v[0:64], before)
    temporal = [
        (t_own[0:64] + t_after) * 0.125,
        (t_own[0:64] + t_own[64:128]) * 0.125,
        (t_own[64:128] + t_before) * 0.125,
    ]
    for k in range(3):
        partf[4 * k : 4 * k + 4] = temporal[k].reshape(4, 16, 256)
    spatial = dot_nt(q_v[0], g_v[0]) + dot_nt(q_v[1], g_v[1])
    partf[12:48] = spatial.reshape(36, 16, 256)
    part[...] = partf[...].astype(BF)

    mine = pl.ds(core * UNITS, UNITS)
    theirs = pl.ds((1 - core) * UNITS, UNITS)
    exchange = remote(part.at[theirs], xch, xch_send, xch_recv, sibling)
    exchange.start()

    def input_products(f):
        p_v[...] = dot(sw_v[...].reshape(576, 256), g_v[f]).reshape(9, 64, 512)

    cell = lax.broadcasted_iota(jnp.int32, (16, 512), 1)

    def input_parities(f):
        def tile(i, carry):
            here = pl.ds(pl.multiple_of(16 * i, 16), 16)
            tops, bottoms = [], []
            for b in range(3):
                t0, t1, t2 = p_v[b, here, :], p_v[3 + b, here, :], p_v[6 + b, here, :]
                tops.append(t0 + t1 + jnp.where(cell >= 64, pltpu.roll(t2, 64, 1), 0.0))
                bottoms.append(t1 + t2 + jnp.where(cell < 448, pltpu.roll(t0, 448, 1), 0.0))
            for r, (u0, u1, u2) in enumerate((tops, bottoms)):
                even = u0 + u1 + jnp.where((cell & 63) != 0, pltpu.roll(u2, 1, 1), 0.0)
                odd = u1 + u2 + jnp.where((cell & 63) != 63, pltpu.roll(u0, 511, 1), 0.0)
                for j in range(4):
                    cut = slice(128 * j, 128 * j + 128)
                    xe_v[r, j, here, 0:128] = even[:, cut].astype(BF)
                    xe_v[r, j, here, 128:256] = odd[:, cut].astype(BF)
            return carry

        lax.fori_loop(0, 4, tile, 0)

    k_of = lax.broadcasted_iota(jnp.int32, (256, 256), 0)
    w_of = lax.broadcasted_iota(jnp.int32, (256, 256), 1)
    place = ((k_of >> 6) & 1) * 128 + 2 * (k_of & 63) + (k_of >> 7)
    weave = jnp.where(w_of == place, 1.0, 0.0).astype(BF)

    def input_output(f):
        woven = dot(xe_v[...].reshape(512, 256), weave).reshape(2, 4, 64, 256)
        for r in range(2):
            for j in range(4):
                for k in range(2):
                    h = 2 * (2 * j + k) + r
                    z_v[pl.ds(h, 64, stride=16), :] = woven[r, j, :, 128 * k : 128 * k + 128]
        out_v[f] = z_v[...].reshape(64, 16, 128).astype(BF)
        copy = pltpu.make_async_copy(out_v.at[f], ig_h.at[f], out_sem.at[f])
        copy.start()
        return copy

    loads[4].wait()
    input_products(0)

    exchange.wait_recv()
    half_v[...] = (partf[mine] + xch[...].astype(F32)).astype(BF)

    def owner_loop(body):
        def group(g, carry):
            for r in range(3):
                body(3 * g + r, 4 * g + r + core)
            return carry

        lax.fori_loop(0, 8, group, 0)

    def scatter(unit, owner):
        @pl.when(owner != chip)
        def _():
            slot = lax.rem(chip - owner + 63, CHIPS)
            remote(
                half_v.at[unit], rs_v.at[slot], rs_send, rs_recv, (2 * owner + core, c)
            ).start()

    owner_loop(scatter)

    place_in_group = lax.rem(chip, 4) - core
    is_owner = jnp.logical_and(place_in_group >= 0, place_in_group < 3)
    my_unit = 3 * lax.div(chip, 4) + place_in_group

    input_parities(0)
    out_copies = [input_output(0)]

    @pl.when(is_owner)
    def _():
        dst = rs_v.at[pl.ds(0, CHIPS - 1)]
        pltpu.make_async_copy(dst, dst, rs_recv).wait()
        total = half_v[my_unit].astype(F32)
        for slot in range(CHIPS - 1):
            total = total + rs_v[slot].astype(F32)
        gr_v[core * UNITS + my_unit] = total.astype(BF)

        def spread(j, carry):
            src = gr_v.at[core * UNITS + my_unit]
            device = (2 * lax.rem(chip + j, CHIPS) + core, c)
            remote(src, src, ag_send, ag_recv, device).start()
            return carry

        lax.fori_loop(1, CHIPS, spread, 0)

    input_products(1)
    input_parities(1)
    out_copies.append(input_output(1))

    @pl.when(is_owner)
    def _():
        dst = gr_v.at[pl.ds(0, UNITS - 1)]
        pltpu.make_async_copy(dst, dst, ag_recv).wait()

    @pl.when(jnp.logical_not(is_owner))
    def _():
        dst = gr_v.at[pl.ds(0, UNITS)]
        pltpu.make_async_copy(dst, dst, ag_recv).wait()

    handover = remote(gr_v.at[mine], gr_v.at[mine], sib_send, sib_recv, sibling)
    handover.start()

    for copy in sent:
        copy.wait_send()

    @pl.when(to_ok)
    def _():
        for copy in others:
            copy.wait_send()

    exchange.wait_send()

    @pl.when(is_owner)
    def _():
        src = half_v.at[pl.ds(0, UNITS - 1)]
        pltpu.make_async_copy(src, src, rs_send).wait()
        src = rs_v.at[pl.ds(0, CHIPS - 1)]
        pltpu.make_async_copy(src, src, ag_send).wait()

    @pl.when(jnp.logical_not(is_owner))
    def _():
        src = half_v.at[pl.ds(0, UNITS)]
        pltpu.make_async_copy(src, src, rs_send).wait()

    for copy in out_copies:
        copy.wait()
    handover.wait()


def shards(inputs, saved, cotangent, spatial_w, temporal_w):
    scale = 1.0 / math.sqrt(128 * 16 * 128)
    vmem = pltpu.VMEM
    dma = pltpu.SemaphoreType.DMA
    input_grad, grads = pl.pallas_call(
        kernel,
        out_shape=(
            jax.ShapeDtypeStruct((2, 64, 16, 128), BF),
            jax.ShapeDtypeStruct((2 * UNITS, 16, 256), BF),
        ),
        in_specs=[pl.BlockSpec(memory_space=pl.ANY)] * 5,
        out_specs=(
            pl.BlockSpec(memory_space=pl.ANY),
            pl.BlockSpec(memory_space=pltpu.VMEM),
        ),
        scratch_shapes=[
            vmem((2, 64, 16, 128), BF),
            vmem((2, 64, 16, 128), BF),
            vmem((3, 3, 64, 256), BF),
            vmem((3, 256, 256), BF),
            vmem((2, 4, 64, 512), BF),
            vmem((2, 4, 64, 512), BF),
            vmem((4, 2048, 128), F32),
            vmem((2, 576, 512), BF),
            vmem((128, 512), BF),
            vmem((768, 512), F32),
            vmem((2, 256, 512), BF),
            vmem((9, 64, 512), F32),
            vmem((2, 4, 64, 256), BF),
            vmem((1024, 128), F32),
            vmem((2, 64, 16, 128), BF),
            vmem((2 * UNITS, 16, 256), F32),
            vmem((2 * UNITS, 16, 256), BF),
            vmem((UNITS, 16, 256), BF),
            vmem((UNITS, 16, 256), BF),
            vmem((CHIPS - 1, 16, 256), BF),
            dma((5,)),
            dma((2, 4, 2)),
            dma((2, 4, 2)),
            dma((8,)),
            dma((2,)),
            dma, dma,
            dma, dma,
            dma, dma,
            dma, dma,
            dma((2,)),
        ],
        compiler_params=pltpu.CompilerParams(
            collective_id=0, has_side_effects=True, vmem_limit_bytes=56 * 1024 * 1024
        ),
        name="space_time_backward",
    )(inputs, saved, cotangent, spatial_w, temporal_w)
    grads = grads.reshape(12, 64, 256).astype(F32) * scale
    return (input_grad, grads[3:].reshape(3, 3, 64, 256), grads[:3])


def solution(mesh):
    return jax.shard_map(
        shards,
        mesh=mesh,
        in_specs=(
            P("frames", "chan", None, None),
            P("frames", "chan", None, None),
            P("frames", "chan", None),
            P(None, None, "chan", None),
            P(),
        ),
        out_specs=(
            P("frames", "chan", None, None),
            P(None, None, "chan", None),
            P(None, "chan", None),
        ),
        check_vma=False,
    )
```

```python
import math

import jax
import jax.numpy as jnp
from jax import lax
from jax.experimental import pallas as pl
from jax.experimental.pallas import tpu as pltpu
from jax.sharding import PartitionSpec as P

BF = jnp.bfloat16
F32 = jnp.float32
CHIPS = 32
UNITS = 24


FAR_FIRST = sorted(
    [(i, j, k) for i in range(4) for j in range(4) for k in range(2) if i or j or k],
    key=lambda s: -(min(s[0], 4 - s[0]) + min(s[1], 4 - s[1]) + s[2]),
)


def dot(a, b):
    return jnp.dot(a, b, preferred_element_type=F32)


def dot_nt(a, b):
    return lax.dot_general(a, b, (((1,), (1,)), ((), ())), preferred_element_type=F32)


def kernel(
    x_h, s_h, c_h, sw_h, tw_h,
    ig_v, gr_v,
    x_v, s_v, sw_v, tw_v, ring, halo, pool, q_v, sq_v, a_v, g_v, p_v, xe_v, z_v,
    partf, part, xch, half_v, rs_v,
    load_sem, ring_send_sem, ring_recv, fwd_send, halo_recv,
    xch_send, xch_recv, rs_send, rs_recv, ag_send, ag_recv, sib_send, sib_recv,
):
    p = lax.axis_index("frames")
    c = lax.axis_index("chan")
    core = lax.rem(p, 2)
    chip = lax.div(p, 2)
    zl = lax.rem(chip, 2)
    column = lax.div(chip, 2)
    z = 2 * c + zl

    def in_ring(step):
        zz = lax.rem(z + step + 8, 8)
        return (4 * column + 2 * lax.rem(zz, 2) + core, lax.div(zz, 2))

    pair = p + 2 * core - 1
    paired = jnp.logical_and(pair >= 0, pair < 64)

    def in_pair(step):
        zz = lax.rem(z + step + 8, 8)
        return (4 * lax.div(pair, 4) + 2 * lax.rem(zz, 2) + 1 - core, lax.div(zz, 2))

    sibling = (p + 1 - 2 * core, c)

    barrier = pltpu.get_barrier_semaphore()

    def greet(device):
        pl.semaphore_signal(barrier, inc=1, device_id=device, device_id_type=pl.DeviceIdType.MESH)

    greet(in_ring(2))
    greet(in_ring(-2))
    greet(sibling)

    @pl.when(paired)
    def _():
        greet(in_pair(1))
        greet(in_pair(-1))

    x, y = lax.div(chip, 8), lax.rem(column, 4)

    def chip_at(offset):
        return 8 * lax.rem(x + offset[0], 4) + 2 * lax.rem(y + offset[1], 4) + lax.rem(zl + offset[2], 2)

    def greet_chip(j, carry):
        greet((2 * lax.rem(chip + j, CHIPS) + core, c))
        return carry

    lax.fori_loop(1, CHIPS, greet_chip, 0)

    loads = [
        pltpu.make_async_copy(c_h.at[0], ring.at[c], load_sem.at[0]),
        pltpu.make_async_copy(s_h, s_v, load_sem.at[1]),
        pltpu.make_async_copy(x_h, x_v, load_sem.at[2]),
        pltpu.make_async_copy(tw_h, tw_v, load_sem.at[3]),
        pltpu.make_async_copy(sw_h, sw_v, load_sem.at[4]),
    ]
    for load in loads:
        load.start()

    pl.semaphore_wait(barrier, 34 + jnp.where(paired, 2, 0))

    def remote(src, dst, send, recv, device):
        return pltpu.make_async_remote_copy(
            src_ref=src, dst_ref=dst, send_sem=send, recv_sem=recv,
            device_id=device, device_id_type=pl.DeviceIdType.MESH,
        )

    sent = []

    def rows(half):
        return pl.ds(32 * half, 32)

    quarters = {step: lax.rem(c + step + 4, 4) for step in (-1, 0, 1, 2)}

    def ring_send(hop, quarter, half, index, src=None):
        copy = remote(
            ring.at[quarter, rows(half)] if src is None else src, ring.at[quarter, rows(half)],
            ring_send_sem.at[index], ring_recv.at[index], in_ring(hop),
        )
        copy.start()
        sent.append(copy)

    def ring_wait(quarter, half, index):
        dst = ring.at[quarter, rows(half)]
        remote(dst, dst, ring_send_sem.at[index], ring_recv.at[index], sibling).wait_recv()

    def to_sibling(src, quarter, index):
        copy = remote(src, halo.at[core, quarter], fwd_send.at[index], halo_recv.at[0], sibling)
        copy.start()
        sent.append(copy)

    pair_copies = []

    def to_pair(step, src, quarter, index):
        copy = remote(
            src, halo.at[1 - core, quarter], fwd_send.at[index], halo_recv.at[1], in_pair(step)
        )

        @pl.when(paired)
        def _():
            copy.start()

        pair_copies.append(copy)

    for half in range(2):
        ring_send(2, c, half, half, c_h.at[0, rows(half)])
        ring_send(-2, c, half, 2 + half, c_h.at[0, rows(half)])
    to_pair(1, c_h.at[0], c, 4)
    to_pair(-1, c_h.at[0], c, 5)
    to_sibling(c_h.at[0], c, 0)

    def near_shards():
        ring_wait(quarters[-1], 0, 0)
        ring_send(2, quarters[-1], 0, 4)
        ring_wait(quarters[1], 0, 2)
        ring_wait(quarters[1], 1, 3)
        ring_send(-2, quarters[1], 1, 5)
        ring_wait(quarters[-1], 1, 1)
        to_pair(1, ring.at[quarters[-1]], quarters[-1], 6)
        to_pair(-1, ring.at[quarters[1]], quarters[1], 7)
        to_sibling(ring.at[quarters[-1]], quarters[-1], 1)
        to_sibling(ring.at[quarters[1]], quarters[1], 2)

    def far_shard():
        ring_wait(quarters[2], 0, 4)
        ring_wait(quarters[2], 1, 5)
        to_sibling(ring.at[quarters[2]], quarters[2], 3)

    lane = lax.broadcasted_iota(jnp.int32, (128, 384), 1)
    column_of = lax.broadcasted_iota(jnp.int32, (128, 384), 0)
    first = 2 * (lane & 63) + (lane >> 7) - 1
    pairs = jnp.where(
        jnp.logical_or(column_of == first, column_of == first + 1), 1.0, 0.0
    ).astype(BF)
    low = lax.broadcasted_iota(jnp.int32, (64, 128), 1) < 64

    loads[1].wait()
    for f in range(2):
        pool[0, pl.ds(f * 1024, 1024), :] = dot(
            s_v[f].reshape(1024, 128), pairs[:, 128:256]
        )
        height = [pool[0, pl.ds(f * 1024 + h, 64, stride=16), :] for h in range(16)]
        for j in range(4):
            upper = height[4 * j] + height[4 * j + 1]
            lower = height[4 * j + 2] + height[4 * j + 3]
            sq_v[pl.ds(64 * f, 64), 128 * j : 128 * j + 128] = jnp.where(low, upper, lower).astype(BF)

    loads[2].wait()
    for f in range(2):
        sums = dot(x_v[f].reshape(1024, 128), pairs)
        for b in range(3):
            pool[1 + b, pl.ds(f * 1024, 1024), :] = sums[:, 128 * b : 128 * b + 128]
    near_shards()
    for f in range(2):
        for b in range(3):
            height = [pool[1 + b, pl.ds(f * 1024 + h, 64, stride=16), :] for h in range(16)]
            total = (
                [height[0]] + [height[h] + height[h + 1] for h in range(15)] + [height[15]]
            )
            for a in range(3):
                for j in range(4):
                    q_v[f, pl.ds((3 * a + b) * 64, 64), 128 * j : 128 * j + 128] = jnp.where(
                        low, total[4 * j + a], total[4 * j + a + 2]
                    ).astype(BF)
    loads[0].wait()
    loads[3].wait()
    far_shard()

    own = ring[...].reshape(256, 512)
    a_v[...] = dot(tw_v[...].reshape(768, 256), own)
    t_own = dot_nt(sq_v[...], own)

    dst = halo.at[1 - core]
    pltpu.make_async_copy(dst, dst, halo_recv.at[0]).wait()

    @pl.when(paired)
    def _():
        dst = halo.at[core]
        pltpu.make_async_copy(dst, dst, halo_recv.at[1]).wait()

    @pl.when(jnp.logical_not(paired))
    def _():
        halo[core] = jnp.zeros((4, 64, 512), BF)

    before = halo[0].reshape(256, 512)
    after = halo[1].reshape(256, 512)
    middle = a_v[256:512]
    g_v[0] = ((a_v[0:256] + middle + dot(tw_v[2], before)) * 0.125).astype(BF)
    g_v[1] = ((dot(tw_v[0], after) + middle + a_v[512:768]) * 0.125).astype(BF)

    t_after = dot_nt(sq_v[64:128], after)
    t_before = dot_nt(sq_v[0:64], before)
    temporal = [
        (t_own[0:64] + t_after) * 0.125,
        (t_own[0:64] + t_own[64:128]) * 0.125,
        (t_own[64:128] + t_before) * 0.125,
    ]
    for k in range(3):
        partf[4 * k : 4 * k + 4] = temporal[k].reshape(4, 16, 256)
    spatial = dot_nt(q_v[0], g_v[0]) + dot_nt(q_v[1], g_v[1])
    partf[12:48] = spatial.reshape(36, 16, 256)
    part[...] = partf[...].astype(BF)

    mine = pl.ds(core * UNITS, UNITS)
    theirs = pl.ds((1 - core) * UNITS, UNITS)
    exchange = remote(part.at[theirs], xch, xch_send, xch_recv, sibling)
    exchange.start()

    def input_products(f):
        p_v[...] = dot(sw_v[...].reshape(576, 256), g_v[f]).reshape(9, 64, 512)

    cell = lax.broadcasted_iota(jnp.int32, (16, 512), 1)

    def input_parities(f):
        def tile(i, carry):
            here = pl.ds(pl.multiple_of(16 * i, 16), 16)
            tops, bottoms = [], []
            for b in range(3):
                t0, t1, t2 = p_v[b, here, :], p_v[3 + b, here, :], p_v[6 + b, here, :]
                tops.append(t0 + t1 + jnp.where(cell >= 64, pltpu.roll(t2, 64, 1), 0.0))
                bottoms.append(t1 + t2 + jnp.where(cell < 448, pltpu.roll(t0, 448, 1), 0.0))
            for r, (u0, u1, u2) in enumerate((tops, bottoms)):
                even = u0 + u1 + jnp.where((cell & 63) != 0, pltpu.roll(u2, 1, 1), 0.0)
                odd = u1 + u2 + jnp.where((cell & 63) != 63, pltpu.roll(u0, 511, 1), 0.0)
                for j in range(4):
                    cut = slice(128 * j, 128 * j + 128)
                    xe_v[r, j, here, 0:128] = even[:, cut].astype(BF)
                    xe_v[r, j, here, 128:256] = odd[:, cut].astype(BF)
            return carry

        lax.fori_loop(0, 4, tile, 0)

    k_of = lax.broadcasted_iota(jnp.int32, (256, 256), 0)
    w_of = lax.broadcasted_iota(jnp.int32, (256, 256), 1)
    place = ((k_of >> 6) & 1) * 128 + 2 * (k_of & 63) + (k_of >> 7)
    weave = jnp.where(w_of == place, 1.0, 0.0).astype(BF)

    def input_output(f):
        woven = dot(xe_v[...].reshape(512, 256), weave).reshape(2, 4, 64, 256)
        for r in range(2):
            for j in range(4):
                for k in range(2):
                    h = 2 * (2 * j + k) + r
                    z_v[pl.ds(h, 64, stride=16), :] = woven[r, j, :, 128 * k : 128 * k + 128]
        ig_v[f] = z_v[...].reshape(64, 16, 128).astype(BF)

    loads[4].wait()
    input_products(0)

    exchange.wait_recv()
    half_v[...] = (partf[mine] + xch[...].astype(F32)).astype(BF)

    for slot, offset in enumerate(FAR_FIRST):
        owner = chip_at(offset)
        owner_place = lax.rem(owner, 4) - core

        @pl.when(jnp.logical_and(owner_place >= 0, owner_place < 3))
        def _():
            unit = 3 * lax.div(owner, 4) + owner_place
            remote(
                half_v.at[unit], rs_v.at[slot], rs_send, rs_recv, (2 * owner + core, c)
            ).start()

    place_in_group = lax.rem(chip, 4) - core
    is_owner = jnp.logical_and(place_in_group >= 0, place_in_group < 3)
    my_unit = 3 * lax.div(chip, 4) + place_in_group

    input_parities(0)
    input_output(0)

    @pl.when(is_owner)
    def _():
        dst = rs_v.at[pl.ds(0, CHIPS - 1)]
        pltpu.make_async_copy(dst, dst, rs_recv).wait()
        total = half_v[my_unit].astype(F32)
        for slot in range(CHIPS - 1):
            total = total + rs_v[slot].astype(F32)
        gr_v[core * UNITS + my_unit] = total.astype(BF)

        for offset in FAR_FIRST:
            src = gr_v.at[core * UNITS + my_unit]
            remote(src, src, ag_send, ag_recv, (2 * chip_at(offset) + core, c)).start()

    input_products(1)
    input_parities(1)
    input_output(1)

    @pl.when(is_owner)
    def _():
        dst = gr_v.at[pl.ds(0, UNITS - 1)]
        pltpu.make_async_copy(dst, dst, ag_recv).wait()

    @pl.when(jnp.logical_not(is_owner))
    def _():
        dst = gr_v.at[pl.ds(0, UNITS)]
        pltpu.make_async_copy(dst, dst, ag_recv).wait()

    handover = remote(gr_v.at[mine], gr_v.at[mine], sib_send, sib_recv, sibling)
    handover.start()

    for copy in sent:
        copy.wait_send()

    @pl.when(paired)
    def _():
        for copy in pair_copies:
            copy.wait_send()

    exchange.wait_send()

    @pl.when(is_owner)
    def _():
        src = half_v.at[pl.ds(0, UNITS - 1)]
        pltpu.make_async_copy(src, src, rs_send).wait()
        src = rs_v.at[pl.ds(0, CHIPS - 1)]
        pltpu.make_async_copy(src, src, ag_send).wait()

    @pl.when(jnp.logical_not(is_owner))
    def _():
        src = half_v.at[pl.ds(0, UNITS)]
        pltpu.make_async_copy(src, src, rs_send).wait()

    handover.wait()


def finish(ig_v, gr_v, ig_out, sp_out, te_out, wide_v, sem):
    scale = 1.0 / math.sqrt(128 * 16 * 128)
    stores = [pltpu.make_async_copy(ig_v, ig_out, sem.at[4])]
    stores[0].start()
    for k in range(4):
        wide_v[12 * k : 12 * k + 12] = gr_v[12 * k : 12 * k + 12].astype(F32) * scale
        dst = te_out if k == 0 else sp_out.at[pl.ds(12 * k - 12, 12)]
        store = pltpu.make_async_copy(wide_v.at[pl.ds(12 * k, 12)], dst, sem.at[k])
        store.start()
        stores.append(store)
    for store in stores:
        store.wait()


def shards(inputs, saved, cotangent, spatial_w, temporal_w):
    vmem = pltpu.VMEM
    dma = pltpu.SemaphoreType.DMA
    input_grad, grads = pl.pallas_call(
        kernel,
        out_shape=(
            pltpu.VMEM((2, 64, 16, 128), BF),
            pltpu.VMEM((2 * UNITS, 16, 256), BF),
        ),
        in_specs=[pl.BlockSpec(memory_space=pl.ANY)] * 5,
        out_specs=(
            pl.BlockSpec(memory_space=pltpu.VMEM),
            pl.BlockSpec(memory_space=pltpu.VMEM),
        ),
        scratch_shapes=[
            vmem((2, 64, 16, 128), BF),
            vmem((2, 64, 16, 128), BF),
            vmem((3, 3, 64, 256), BF),
            vmem((3, 256, 256), BF),
            vmem((4, 64, 512), BF),
            vmem((2, 4, 64, 512), BF),
            vmem((4, 2048, 128), F32),
            vmem((2, 576, 512), BF),
            vmem((128, 512), BF),
            vmem((768, 512), F32),
            vmem((2, 256, 512), BF),
            vmem((9, 64, 512), F32),
            vmem((2, 4, 64, 256), BF),
            vmem((1024, 128), F32),
            vmem((2 * UNITS, 16, 256), F32),
            vmem((2 * UNITS, 16, 256), BF),
            vmem((UNITS, 16, 256), BF),
            vmem((UNITS, 16, 256), BF),
            vmem((CHIPS - 1, 16, 256), BF),
            dma((5,)),
            dma((6,)),
            dma((6,)),
            dma((8,)),
            dma((2,)),
            dma, dma,
            dma, dma,
            dma, dma,
            dma, dma,
        ],
        compiler_params=pltpu.CompilerParams(
            collective_id=0, has_side_effects=True, vmem_limit_bytes=56 * 1024 * 1024
        ),
        name="space_time_backward",
    )(inputs, saved, cotangent, spatial_w, temporal_w)
    input_grad = pltpu.with_memory_space_constraint(input_grad, pltpu.VMEM)
    grads = pltpu.with_memory_space_constraint(grads, pltpu.VMEM)
    input_grad, spatial, temporal = pl.pallas_call(
        finish,
        out_shape=(
            jax.ShapeDtypeStruct((2, 64, 16, 128), BF),
            jax.ShapeDtypeStruct((36, 16, 256), F32),
            jax.ShapeDtypeStruct((12, 16, 256), F32),
        ),
        in_specs=[pl.BlockSpec(memory_space=pltpu.VMEM)] * 2,
        out_specs=[pl.BlockSpec(memory_space=pl.ANY)] * 3,
        scratch_shapes=[
            vmem((2 * UNITS, 16, 256), F32),
            dma((5,)),
        ],
        name="scale_gradients",
    )(input_grad, grads)
    return (input_grad, spatial.reshape(3, 3, 64, 256), temporal.reshape(3, 64, 256))


def solution(mesh):
    return jax.shard_map(
        shards,
        mesh=mesh,
        in_specs=(
            P("frames", "chan", None, None),
            P("frames", "chan", None, None),
            P("frames", "chan", None),
            P(None, None, "chan", None),
            P(),
        ),
        out_specs=(
            P("frames", "chan", None, None),
            P(None, None, "chan", None),
            P(None, "chan", None),
        ),
        check_vma=False,
    )
```

```python
import math

import jax
import jax.numpy as jnp
from jax import lax
from jax.experimental import pallas as pl
from jax.experimental.pallas import tpu as pltpu
from jax.sharding import PartitionSpec as P

BF = jnp.bfloat16
F32 = jnp.float32
CHIPS = 32
PIECES = 48


FAR_FIRST = sorted(
    [(i, j, k) for i in range(4) for j in range(4) for k in range(2) if i or j or k],
    key=lambda s: -(min(s[0], 4 - s[0]) + min(s[1], 4 - s[1]) + s[2]),
)


NEXT = [(1, 0, 0), (3, 0, 0), (0, 1, 0), (0, 3, 0), (0, 0, 1)]
ROUNDS = 4


def dot(a, b):
    return jnp.dot(a, b, preferred_element_type=F32)


def dot_nt(a, b):
    return lax.dot_general(a, b, (((1,), (1,)), ((), ())), preferred_element_type=F32)


def kernel(
    x_h, s_h, c_h, sw_h, tw_h,
    ig_v, gr_v,
    x_v, s_v, sw_v, tw_v, ring, halo, pool, q_v, sq_v, a_v, g_v, p_v, xe_v, z_v,
    given, kept, xch, half_v, rs_v,
    load_sem, ring_send_sem, ring_recv, fwd_send, halo_recv,
    xch_send, xch_recv, rs_send, rs_recv, ag_send, ag_recv, sib_send, sib_recv, news,
):
    p = lax.axis_index("frames")
    c = lax.axis_index("chan")
    core = lax.rem(p, 2)
    chip = lax.div(p, 2)
    zl = lax.rem(chip, 2)
    column = lax.div(chip, 2)
    z = 2 * c + zl

    def in_ring(step):
        zz = lax.rem(z + step + 8, 8)
        return (4 * column + 2 * lax.rem(zz, 2) + core, lax.div(zz, 2))

    pair = p + 2 * core - 1
    paired = jnp.logical_and(pair >= 0, pair < 64)

    def in_pair(step):
        zz = lax.rem(z + step + 8, 8)
        return (4 * lax.div(pair, 4) + 2 * lax.rem(zz, 2) + 1 - core, lax.div(zz, 2))

    sibling = (p + 1 - 2 * core, c)

    barrier = pltpu.get_barrier_semaphore()

    def greet(device):
        pl.semaphore_signal(barrier, inc=1, device_id=device, device_id_type=pl.DeviceIdType.MESH)

    greet(in_ring(2))
    greet(in_ring(-2))
    greet(sibling)

    @pl.when(paired)
    def _():
        greet(in_pair(1))
        greet(in_pair(-1))

    x, y = lax.div(chip, 8), lax.rem(column, 4)

    def chip_at(offset):
        return 8 * lax.rem(x + offset[0], 4) + 2 * lax.rem(y + offset[1], 4) + lax.rem(zl + offset[2], 2)

    for offset in NEXT:
        greet((2 * chip_at(offset) + core, c))

    loads = [
        pltpu.make_async_copy(c_h.at[0], ring.at[c], load_sem.at[0]),
        pltpu.make_async_copy(s_h, s_v, load_sem.at[1]),
        pltpu.make_async_copy(x_h, x_v, load_sem.at[2]),
        pltpu.make_async_copy(tw_h, tw_v, load_sem.at[3]),
        pltpu.make_async_copy(sw_h, sw_v, load_sem.at[4]),
    ]
    for load in loads:
        load.start()

    pl.semaphore_wait(barrier, 3 + len(NEXT) + jnp.where(paired, 2, 0))
    loads[0].wait()

    def remote(src, dst, send, recv, device):
        return pltpu.make_async_remote_copy(
            src_ref=src, dst_ref=dst, send_sem=send, recv_sem=recv,
            device_id=device, device_id_type=pl.DeviceIdType.MESH,
        )

    sent = []

    def rows(half):
        return pl.ds(32 * half, 32)

    quarters = {step: lax.rem(c + step + 4, 4) for step in (-1, 0, 1, 2)}

    def ring_send(hop, quarter, half, index, src=None):
        copy = remote(
            ring.at[quarter, rows(half)] if src is None else src, ring.at[quarter, rows(half)],
            ring_send_sem.at[index], ring_recv.at[index], in_ring(hop),
        )
        copy.start()
        sent.append(copy)

    def ring_wait(quarter, half, index):
        dst = ring.at[quarter, rows(half)]
        remote(dst, dst, ring_send_sem.at[index], ring_recv.at[index], sibling).wait_recv()

    def to_sibling(src, quarter, index):
        copy = remote(src, halo.at[core, quarter], fwd_send.at[index], halo_recv.at[0], sibling)
        copy.start()
        sent.append(copy)

    pair_copies = []

    def to_pair(step, src, quarter, index):
        copy = remote(
            src, halo.at[1 - core, quarter], fwd_send.at[index], halo_recv.at[1], in_pair(step)
        )

        @pl.when(paired)
        def _():
            copy.start()

        pair_copies.append(copy)

    for half in range(2):
        ring_send(2, c, half, half, ring.at[c, rows(half)])
        ring_send(-2, c, half, 2 + half, ring.at[c, rows(half)])
    to_pair(1, ring.at[c], c, 4)
    to_pair(-1, ring.at[c], c, 5)
    to_sibling(ring.at[c], c, 0)

    def near_shards():
        ring_wait(quarters[-1], 0, 0)
        ring_send(2, quarters[-1], 0, 4)
        ring_wait(quarters[1], 0, 2)
        ring_wait(quarters[1], 1, 3)
        ring_send(-2, quarters[1], 1, 5)
        ring_wait(quarters[-1], 1, 1)
        to_pair(1, ring.at[quarters[-1]], quarters[-1], 6)
        to_pair(-1, ring.at[quarters[1]], quarters[1], 7)
        to_sibling(ring.at[quarters[-1]], quarters[-1], 1)
        to_sibling(ring.at[quarters[1]], quarters[1], 2)

    def far_shard():
        ring_wait(quarters[2], 0, 4)
        ring_wait(quarters[2], 1, 5)
        to_sibling(ring.at[quarters[2]], quarters[2], 3)

    def spread_news(k):
        for offset in NEXT:
            pl.semaphore_signal(
                news.at[k], inc=1, device_id=(2 * chip_at(offset) + core, c),
                device_id_type=pl.DeviceIdType.MESH,
            )

    def hear_news(k):
        pl.semaphore_wait(news.at[k], len(NEXT))

    spread_news(0)

    lane = lax.broadcasted_iota(jnp.int32, (128, 384), 1)
    column_of = lax.broadcasted_iota(jnp.int32, (128, 384), 0)
    first = 2 * (lane & 63) + (lane >> 7) - 1
    pairs = jnp.where(
        jnp.logical_or(column_of == first, column_of == first + 1), 1.0, 0.0
    ).astype(BF)
    low = lax.broadcasted_iota(jnp.int32, (64, 128), 1) < 64

    loads[1].wait()
    for f in range(2):
        pool[0, pl.ds(f * 1024, 1024), :] = dot(
            s_v[f].reshape(1024, 128), pairs[:, 128:256]
        )
        height = [pool[0, pl.ds(f * 1024 + h, 64, stride=16), :] for h in range(16)]
        for j in range(4):
            upper = height[4 * j] + height[4 * j + 1]
            lower = height[4 * j + 2] + height[4 * j + 3]
            sq_v[pl.ds(64 * f, 64), 128 * j : 128 * j + 128] = jnp.where(low, upper, lower).astype(BF)

    hear_news(0)
    spread_news(1)
    loads[2].wait()
    for f in range(2):
        sums = dot(x_v[f].reshape(1024, 128), pairs)
        for b in range(3):
            pool[1 + b, pl.ds(f * 1024, 1024), :] = sums[:, 128 * b : 128 * b + 128]
    hear_news(1)
    spread_news(2)
    near_shards()
    for f in range(2):
        for b in range(3):
            height = [pool[1 + b, pl.ds(f * 1024 + h, 64, stride=16), :] for h in range(16)]
            total = (
                [height[0]] + [height[h] + height[h + 1] for h in range(15)] + [height[15]]
            )
            for a in range(3):
                for j in range(4):
                    q_v[f, pl.ds((3 * a + b) * 64, 64), 128 * j : 128 * j + 128] = jnp.where(
                        low, total[4 * j + a], total[4 * j + a + 2]
                    ).astype(BF)
    loads[3].wait()
    hear_news(2)
    spread_news(3)
    far_shard()

    own = ring[...].reshape(256, 512)
    a_v[...] = dot(tw_v[...].reshape(768, 256), own)
    t_own = dot_nt(sq_v[...], own)

    dst = halo.at[1 - core]
    pltpu.make_async_copy(dst, dst, halo_recv.at[0]).wait()

    @pl.when(paired)
    def _():
        dst = halo.at[core]
        pltpu.make_async_copy(dst, dst, halo_recv.at[1]).wait()

    @pl.when(jnp.logical_not(paired))
    def _():
        halo[core] = jnp.zeros((4, 64, 512), BF)

    before = halo[0].reshape(256, 512)
    after = halo[1].reshape(256, 512)
    middle = a_v[256:512]
    g_v[0] = ((a_v[0:256] + middle + dot(tw_v[2], before)) * 0.125).astype(BF)
    g_v[1] = ((dot(tw_v[0], after) + middle + a_v[512:768]) * 0.125).astype(BF)

    def put(dst, at, value):
        count = value.shape[0] // 16
        for side in range(2):
            piece = value[:, 128 * side : 128 * side + 128].reshape(count, 16, 128)
            dst[at : at + count, side] = piece.astype(dst.dtype)

    def spatial(dst, at, first_tap, last_tap):
        taps = slice(64 * first_tap, 64 * last_tap)
        put(dst, at, dot_nt(q_v[0, taps], g_v[0]) + dot_nt(q_v[1, taps], g_v[1]))

    def lower_half(dst):
        t_after = dot_nt(sq_v[64:128], after)
        t_before = dot_nt(sq_v[0:64], before)
        put(dst, 0, (t_own[0:64] + t_after) * 0.125)
        put(dst, 4, (t_own[0:64] + t_own[64:128]) * 0.125)
        put(dst, 8, (t_own[64:128] + t_before) * 0.125)
        spatial(dst, 12, 0, 3)

    def upper_half(dst):
        spatial(dst, 0, 3, 9)

    exchange = remote(given, xch, xch_send, xch_recv, sibling)

    @pl.when(core == 0)
    def _():
        upper_half(given)
        exchange.start()
        lower_half(kept)

    @pl.when(core == 1)
    def _():
        lower_half(given)
        exchange.start()
        upper_half(kept)

    def input_products(f):
        p_v[...] = dot(sw_v[...].reshape(576, 256), g_v[f]).reshape(9, 64, 512)

    cell = lax.broadcasted_iota(jnp.int32, (16, 512), 1)

    def input_parities(f):
        def tile(i, carry):
            here = pl.ds(pl.multiple_of(16 * i, 16), 16)
            tops, bottoms = [], []
            for b in range(3):
                t0, t1, t2 = p_v[b, here, :], p_v[3 + b, here, :], p_v[6 + b, here, :]
                tops.append(t0 + t1 + jnp.where(cell >= 64, pltpu.roll(t2, 64, 1), 0.0))
                bottoms.append(t1 + t2 + jnp.where(cell < 448, pltpu.roll(t0, 448, 1), 0.0))
            for r, (u0, u1, u2) in enumerate((tops, bottoms)):
                even = u0 + u1 + jnp.where((cell & 63) != 0, pltpu.roll(u2, 1, 1), 0.0)
                odd = u1 + u2 + jnp.where((cell & 63) != 63, pltpu.roll(u0, 511, 1), 0.0)
                for j in range(4):
                    cut = slice(128 * j, 128 * j + 128)
                    xe_v[r, j, here, 0:128] = even[:, cut].astype(BF)
                    xe_v[r, j, here, 128:256] = odd[:, cut].astype(BF)
            return carry

        lax.fori_loop(0, 4, tile, 0)

    k_of = lax.broadcasted_iota(jnp.int32, (256, 256), 0)
    w_of = lax.broadcasted_iota(jnp.int32, (256, 256), 1)
    place = ((k_of >> 6) & 1) * 128 + 2 * (k_of & 63) + (k_of >> 7)
    weave = jnp.where(w_of == place, 1.0, 0.0).astype(BF)

    def input_output(f):
        woven = dot(xe_v[...].reshape(512, 256), weave).reshape(2, 4, 64, 256)
        for r in range(2):
            for j in range(4):
                for k in range(2):
                    h = 2 * (2 * j + k) + r
                    z_v[pl.ds(h, 64, stride=16), :] = woven[r, j, :, 128 * k : 128 * k + 128]
        ig_v[f] = z_v[...].reshape(64, 16, 128).astype(BF)

    exchange.wait_recv()
    half_v[...] = (kept[...] + xch[...].astype(F32)).astype(BF).reshape(PIECES, 16, 128)
    hear_news(3)

    large = lax.rem(x + y + zl + core, 2) == 0
    large_at, small_at = 2 * column, 32 + column

    for slot, offset in enumerate(FAR_FIRST):
        owner = chip_at(offset)
        owner_column = lax.div(owner, 2)
        owner_large = large if sum(offset) % 2 == 0 else jnp.logical_not(large)

        @pl.when(owner_large)
        def _():
            remote(
                half_v.at[pl.ds(2 * owner_column, 2)], rs_v.at[pl.ds(2 * slot, 2)],
                rs_send, rs_recv, (2 * owner + core, c),
            ).start()

        @pl.when(jnp.logical_not(owner_large))
        def _():
            remote(
                half_v.at[pl.ds(32 + owner_column, 1)], rs_v.at[pl.ds(slot, 1)],
                rs_send, rs_recv, (2 * owner + core, c),
            ).start()

    loads[4].wait()
    input_products(0)
    input_parities(0)
    input_output(0)

    def own_piece(at, count):
        dst = rs_v.at[pl.ds(0, count * (CHIPS - 1))]
        pltpu.make_async_copy(dst, dst, rs_recv).wait()
        total = half_v[pl.ds(at, count)].astype(F32)
        for slot in range(CHIPS - 1):
            total = total + rs_v[count * slot : count * slot + count].astype(F32)
        here = pl.ds(core * PIECES + at, count)
        gr_v[here] = total.astype(BF)
        for offset in FAR_FIRST:
            src = gr_v.at[here]
            remote(src, src, ag_send, ag_recv, (2 * chip_at(offset) + core, c)).start()

    @pl.when(large)
    def _():
        own_piece(large_at, 2)

    @pl.when(jnp.logical_not(large))
    def _():
        own_piece(small_at, 1)

    input_products(1)
    input_parities(1)
    input_output(1)

    def rest(count, sem):
        dst = gr_v.at[pl.ds(0, count)]
        pltpu.make_async_copy(dst, dst, sem).wait()

    @pl.when(large)
    def _():
        rest(PIECES - 2, ag_recv)

    @pl.when(jnp.logical_not(large))
    def _():
        rest(PIECES - 1, ag_recv)

    mine = pl.ds(core * PIECES, PIECES)
    handover = remote(gr_v.at[mine], gr_v.at[mine], sib_send, sib_recv, sibling)
    handover.start()

    for copy in sent:
        copy.wait_send()

    @pl.when(paired)
    def _():
        for copy in pair_copies:
            copy.wait_send()

    exchange.wait_send()

    @pl.when(large)
    def _():
        rest(PIECES - 2, rs_send)
        rest(2 * (CHIPS - 1), ag_send)

    @pl.when(jnp.logical_not(large))
    def _():
        rest(PIECES - 1, rs_send)
        rest(CHIPS - 1, ag_send)

    handover.wait()


def finish(ig_v, gr_v, ig_out, sp_out, te_out, wide_v, sem):
    scale = 1.0 / math.sqrt(128 * 16 * 128)
    stores = [pltpu.make_async_copy(ig_v, ig_out, sem.at[4])]
    stores[0].start()
    for k in range(4):
        pieces = gr_v[24 * k : 24 * k + 24].reshape(12, 2, 16, 128)
        for side in range(2):
            wide_v[12 * k : 12 * k + 12, :, 128 * side : 128 * side + 128] = (
                pieces[:, side].astype(F32) * scale
            )
        dst = te_out if k == 0 else sp_out.at[pl.ds(12 * k - 12, 12)]
        store = pltpu.make_async_copy(wide_v.at[pl.ds(12 * k, 12)], dst, sem.at[k])
        store.start()
        stores.append(store)
    for store in stores:
        store.wait()


def shards(inputs, saved, cotangent, spatial_w, temporal_w):
    vmem = pltpu.VMEM
    dma = pltpu.SemaphoreType.DMA
    input_grad, grads = pl.pallas_call(
        kernel,
        out_shape=(
            pltpu.VMEM((2, 64, 16, 128), BF),
            pltpu.VMEM((2 * PIECES, 16, 128), BF),
        ),
        in_specs=[pl.BlockSpec(memory_space=pl.ANY)] * 5,
        out_specs=(
            pl.BlockSpec(memory_space=pltpu.VMEM),
            pl.BlockSpec(memory_space=pltpu.VMEM),
        ),
        scratch_shapes=[
            vmem((2, 64, 16, 128), BF),
            vmem((2, 64, 16, 128), BF),
            vmem((3, 3, 64, 256), BF),
            vmem((3, 256, 256), BF),
            vmem((4, 64, 512), BF),
            vmem((2, 4, 64, 512), BF),
            vmem((4, 2048, 128), F32),
            vmem((2, 576, 512), BF),
            vmem((128, 512), BF),
            vmem((768, 512), F32),
            vmem((2, 256, 512), BF),
            vmem((9, 64, 512), F32),
            vmem((2, 4, 64, 256), BF),
            vmem((1024, 128), F32),
            vmem((24, 2, 16, 128), BF),
            vmem((24, 2, 16, 128), F32),
            vmem((24, 2, 16, 128), BF),
            vmem((PIECES, 16, 128), BF),
            vmem((2 * (CHIPS - 1), 16, 128), BF),
            dma((5,)),
            dma((6,)),
            dma((6,)),
            dma((8,)),
            dma((2,)),
            dma, dma,
            dma, dma,
            dma, dma,
            dma, dma,
            pltpu.SemaphoreType.REGULAR((ROUNDS,)),
        ],
        compiler_params=pltpu.CompilerParams(
            collective_id=0, has_side_effects=True, vmem_limit_bytes=56 * 1024 * 1024
        ),
        name="space_time_backward",
    )(inputs, saved, cotangent, spatial_w, temporal_w)
    input_grad = pltpu.with_memory_space_constraint(input_grad, pltpu.VMEM)
    grads = pltpu.with_memory_space_constraint(grads, pltpu.VMEM)
    input_grad, spatial, temporal = pl.pallas_call(
        finish,
        out_shape=(
            jax.ShapeDtypeStruct((2, 64, 16, 128), BF),
            jax.ShapeDtypeStruct((36, 16, 256), F32),
            jax.ShapeDtypeStruct((12, 16, 256), F32),
        ),
        in_specs=[pl.BlockSpec(memory_space=pltpu.VMEM)] * 2,
        out_specs=[pl.BlockSpec(memory_space=pl.ANY)] * 3,
        scratch_shapes=[
            vmem((48, 16, 256), F32),
            dma((5,)),
        ],
        name="scale_gradients",
    )(input_grad, grads)
    return (input_grad, spatial.reshape(3, 3, 64, 256), temporal.reshape(3, 64, 256))


def solution(mesh):
    return jax.shard_map(
        shards,
        mesh=mesh,
        in_specs=(
            P("frames", "chan", None, None),
            P("frames", "chan", None, None),
            P("frames", "chan", None),
            P(None, None, "chan", None),
            P(),
        ),
        out_specs=(
            P("frames", "chan", None, None),
            P(None, None, "chan", None),
            P(None, "chan", None),
        ),
        check_vma=False,
    )
```

```python
import math

import jax
import jax.numpy as jnp
from jax import lax
from jax.experimental import pallas as pl
from jax.experimental.pallas import tpu as pltpu
from jax.sharding import PartitionSpec as P

BF = jnp.bfloat16
F32 = jnp.float32
CHIPS = 32
PIECES = 48


FAR_FIRST = sorted(
    [(i, j, k) for i in range(4) for j in range(4) for k in range(2) if i or j or k],
    key=lambda s: -(min(s[0], 4 - s[0]) + min(s[1], 4 - s[1]) + s[2]),
)


NEXT = [(1, 0, 0), (3, 0, 0), (0, 1, 0), (0, 3, 0), (0, 0, 1)]
ROUNDS = 4


def dot(a, b):
    return jnp.dot(a, b, preferred_element_type=F32)


def dot_nt(a, b):
    return lax.dot_general(a, b, (((1,), (1,)), ((), ())), preferred_element_type=F32)


def kernel(
    x_h, s_h, c_h, sw_h, tw_h,
    ig_v, gr_v,
    x_v, s_v, sw_v, tw_v, ring, halo, pool, q_v, sq_v, a_v, g_v, p_v, xe_v, z_v,
    given, kept, xch, half_v, rs_v,
    load_sem, ring_send_sem, ring_recv, fwd_send, halo_recv,
    xch_send, xch_recv, rs_send, rs_recv, ag_send, ag_recv, sib_send, sib_recv, news,
):
    p = lax.axis_index("frames")
    c = lax.axis_index("chan")
    core = lax.rem(p, 2)
    chip = lax.div(p, 2)
    zl = lax.rem(chip, 2)
    column = lax.div(chip, 2)
    z = 2 * c + zl

    def in_ring(step):
        zz = lax.rem(z + step + 8, 8)
        return (4 * column + 2 * lax.rem(zz, 2) + core, lax.div(zz, 2))

    pair = p + 2 * core - 1
    paired = jnp.logical_and(pair >= 0, pair < 64)

    def in_pair(step):
        zz = lax.rem(z + step + 8, 8)
        return (4 * lax.div(pair, 4) + 2 * lax.rem(zz, 2) + 1 - core, lax.div(zz, 2))

    sibling = (p + 1 - 2 * core, c)

    barrier = pltpu.get_barrier_semaphore()

    def greet(device):
        pl.semaphore_signal(barrier, inc=1, device_id=device, device_id_type=pl.DeviceIdType.MESH)

    greet(in_ring(2))
    greet(in_ring(-2))
    greet(sibling)

    @pl.when(paired)
    def _():
        greet(in_pair(1))
        greet(in_pair(-1))

    x, y = lax.div(chip, 8), lax.rem(column, 4)

    def chip_at(offset):
        return 8 * lax.rem(x + offset[0], 4) + 2 * lax.rem(y + offset[1], 4) + lax.rem(zl + offset[2], 2)

    for offset in NEXT:
        greet((2 * chip_at(offset) + core, c))

    loads = [
        pltpu.make_async_copy(c_h.at[0], ring.at[c], load_sem.at[0]),
        pltpu.make_async_copy(s_h, s_v, load_sem.at[1]),
        pltpu.make_async_copy(x_h, x_v, load_sem.at[2]),
        pltpu.make_async_copy(tw_h, tw_v, load_sem.at[3]),
        pltpu.make_async_copy(sw_h, sw_v, load_sem.at[4]),
    ]
    for load in loads:
        load.start()

    pl.semaphore_wait(barrier, 3 + len(NEXT) + jnp.where(paired, 2, 0))
    loads[0].wait()

    def remote(src, dst, send, recv, device):
        return pltpu.make_async_remote_copy(
            src_ref=src, dst_ref=dst, send_sem=send, recv_sem=recv,
            device_id=device, device_id_type=pl.DeviceIdType.MESH,
        )

    sent = []

    def rows(half):
        return pl.ds(32 * half, 32)

    quarters = {step: lax.rem(c + step + 4, 4) for step in (-1, 0, 1, 2)}

    def ring_send(hop, quarter, half, index, src=None):
        copy = remote(
            ring.at[quarter, rows(half)] if src is None else src, ring.at[quarter, rows(half)],
            ring_send_sem.at[index], ring_recv.at[index], in_ring(hop),
        )
        copy.start()
        sent.append(copy)

    def ring_wait(quarter, half, index):
        dst = ring.at[quarter, rows(half)]
        remote(dst, dst, ring_send_sem.at[index], ring_recv.at[index], sibling).wait_recv()

    def to_sibling(src, quarter, index):
        copy = remote(src, halo.at[core, quarter], fwd_send.at[index], halo_recv.at[0], sibling)
        copy.start()
        sent.append(copy)

    pair_copies = []

    def to_pair(step, src, quarter, index, dst=None):
        copy = remote(
            src, halo.at[1 - core, quarter] if dst is None else dst,
            fwd_send.at[index], halo_recv.at[1], in_pair(step),
        )

        @pl.when(paired)
        def _():
            copy.start()

        pair_copies.append(copy)

    def to_pair_half(step, quarter, half, index):
        to_pair(
            step, ring.at[quarter, rows(half)], quarter, index,
            halo.at[1 - core, quarter, rows(half)],
        )

    for half in range(2):
        ring_send(2, c, half, half, ring.at[c, rows(half)])
        ring_send(-2, c, 1 - half, 3 - half, ring.at[c, rows(1 - half)])
    to_pair(1, ring.at[c], c, 4)
    to_pair(-1, ring.at[c], c, 5)
    to_sibling(ring.at[c], c, 0)

    def near_shards():
        below, above = quarters[-1], quarters[1]
        ring_wait(below, 0, 0)
        ring_send(2, below, 0, 4)
        ring_wait(above, 1, 3)
        ring_send(-2, above, 1, 5)
        to_pair_half(1, below, 0, 6)
        to_pair_half(-1, above, 1, 8)
        ring_wait(below, 1, 1)
        to_pair_half(1, below, 1, 7)
        ring_wait(above, 0, 2)
        to_pair_half(-1, above, 0, 9)
        to_sibling(ring.at[below], below, 1)
        to_sibling(ring.at[above], above, 2)

    def far_shard():
        ring_wait(quarters[2], 0, 4)
        ring_wait(quarters[2], 1, 5)
        to_sibling(ring.at[quarters[2]], quarters[2], 3)

    def spread_news(k):
        for offset in NEXT:
            pl.semaphore_signal(
                news.at[k], inc=1, device_id=(2 * chip_at(offset) + core, c),
                device_id_type=pl.DeviceIdType.MESH,
            )

    def hear_news(k):
        pl.semaphore_wait(news.at[k], len(NEXT))

    spread_news(0)

    lane = lax.broadcasted_iota(jnp.int32, (128, 384), 1)
    column_of = lax.broadcasted_iota(jnp.int32, (128, 384), 0)
    first = 2 * (lane & 63) + (lane >> 7) - 1
    pairs = jnp.where(
        jnp.logical_or(column_of == first, column_of == first + 1), 1.0, 0.0
    ).astype(BF)
    low = lax.broadcasted_iota(jnp.int32, (64, 128), 1) < 64

    loads[1].wait()
    for f in range(2):
        pool[0, pl.ds(f * 1024, 1024), :] = dot(
            s_v[f].reshape(1024, 128), pairs[:, 128:256]
        )
        height = [pool[0, pl.ds(f * 1024 + h, 64, stride=16), :] for h in range(16)]
        for j in range(4):
            upper = height[4 * j] + height[4 * j + 1]
            lower = height[4 * j + 2] + height[4 * j + 3]
            sq_v[pl.ds(64 * f, 64), 128 * j : 128 * j + 128] = jnp.where(low, upper, lower).astype(BF)

    loads[2].wait()
    for f in range(2):
        sums = dot(x_v[f].reshape(1024, 128), pairs)
        for b in range(3):
            pool[1 + b, pl.ds(f * 1024, 1024), :] = sums[:, 128 * b : 128 * b + 128]
    hear_news(0)
    spread_news(1)
    near_shards()
    hear_news(1)
    spread_news(2)
    for f in range(2):
        for b in range(3):
            height = [pool[1 + b, pl.ds(f * 1024 + h, 64, stride=16), :] for h in range(16)]
            total = (
                [height[0]] + [height[h] + height[h + 1] for h in range(15)] + [height[15]]
            )
            for a in range(3):
                for j in range(4):
                    q_v[f, pl.ds((3 * a + b) * 64, 64), 128 * j : 128 * j + 128] = jnp.where(
                        low, total[4 * j + a], total[4 * j + a + 2]
                    ).astype(BF)
    loads[3].wait()
    hear_news(2)
    spread_news(3)
    far_shard()

    own = ring[...].reshape(256, 512)
    a_v[...] = dot(tw_v[...].reshape(768, 256), own)
    t_own = dot_nt(sq_v[...], own)

    dst = halo.at[1 - core]
    pltpu.make_async_copy(dst, dst, halo_recv.at[0]).wait()

    @pl.when(paired)
    def _():
        dst = halo.at[core]
        pltpu.make_async_copy(dst, dst, halo_recv.at[1]).wait()

    @pl.when(jnp.logical_not(paired))
    def _():
        halo[core] = jnp.zeros((4, 64, 512), BF)

    before = halo[0].reshape(256, 512)
    after = halo[1].reshape(256, 512)
    middle = a_v[256:512]
    g_v[0] = ((a_v[0:256] + middle + dot(tw_v[2], before)) * 0.125).astype(BF)
    g_v[1] = ((dot(tw_v[0], after) + middle + a_v[512:768]) * 0.125).astype(BF)

    def put(dst, at, value):
        count = value.shape[0] // 16
        for side in range(2):
            piece = value[:, 128 * side : 128 * side + 128].reshape(count, 16, 128)
            dst[at : at + count, side] = piece.astype(dst.dtype)

    def spatial(dst, at, first_tap, last_tap):
        taps = slice(64 * first_tap, 64 * last_tap)
        put(dst, at, dot_nt(q_v[0, taps], g_v[0]) + dot_nt(q_v[1, taps], g_v[1]))

    def lower_half(dst):
        t_after = dot_nt(sq_v[64:128], after)
        t_before = dot_nt(sq_v[0:64], before)
        put(dst, 0, (t_own[0:64] + t_after) * 0.125)
        put(dst, 4, (t_own[0:64] + t_own[64:128]) * 0.125)
        put(dst, 8, (t_own[64:128] + t_before) * 0.125)
        spatial(dst, 12, 0, 3)

    def upper_half(dst):
        spatial(dst, 0, 3, 9)

    exchange = remote(given, xch, xch_send, xch_recv, sibling)

    @pl.when(core == 0)
    def _():
        upper_half(given)
        exchange.start()
        lower_half(kept)

    @pl.when(core == 1)
    def _():
        lower_half(given)
        exchange.start()
        upper_half(kept)

    def input_products(f):
        p_v[...] = dot(sw_v[...].reshape(576, 256), g_v[f]).reshape(9, 64, 512)

    cell = lax.broadcasted_iota(jnp.int32, (16, 512), 1)

    def input_parities(f):
        def tile(i, carry):
            here = pl.ds(pl.multiple_of(16 * i, 16), 16)
            tops, bottoms = [], []
            for b in range(3):
                t0, t1, t2 = p_v[b, here, :], p_v[3 + b, here, :], p_v[6 + b, here, :]
                tops.append(t0 + t1 + jnp.where(cell >= 64, pltpu.roll(t2, 64, 1), 0.0))
                bottoms.append(t1 + t2 + jnp.where(cell < 448, pltpu.roll(t0, 448, 1), 0.0))
            for r, (u0, u1, u2) in enumerate((tops, bottoms)):
                even = u0 + u1 + jnp.where((cell & 63) != 0, pltpu.roll(u2, 1, 1), 0.0)
                odd = u1 + u2 + jnp.where((cell & 63) != 63, pltpu.roll(u0, 511, 1), 0.0)
                for j in range(4):
                    cut = slice(128 * j, 128 * j + 128)
                    xe_v[r, j, here, 0:128] = even[:, cut].astype(BF)
                    xe_v[r, j, here, 128:256] = odd[:, cut].astype(BF)
            return carry

        lax.fori_loop(0, 4, tile, 0)

    k_of = lax.broadcasted_iota(jnp.int32, (256, 256), 0)
    w_of = lax.broadcasted_iota(jnp.int32, (256, 256), 1)
    place = ((k_of >> 6) & 1) * 128 + 2 * (k_of & 63) + (k_of >> 7)
    weave = jnp.where(w_of == place, 1.0, 0.0).astype(BF)

    def input_output(f):
        woven = dot(xe_v[...].reshape(512, 256), weave).reshape(2, 4, 64, 256)
        for r in range(2):
            for j in range(4):
                for k in range(2):
                    h = 2 * (2 * j + k) + r
                    z_v[pl.ds(h, 64, stride=16), :] = woven[r, j, :, 128 * k : 128 * k + 128]
        ig_v[f] = z_v[...].reshape(64, 16, 128).astype(BF)

    exchange.wait_recv()
    half_v[...] = (kept[...] + xch[...].astype(F32)).astype(BF).reshape(PIECES, 16, 128)
    hear_news(3)

    large = lax.rem(x + y + zl + core, 2) == 0
    large_at, small_at = 2 * column, 32 + column

    for slot, offset in enumerate(FAR_FIRST):
        owner = chip_at(offset)
        owner_column = lax.div(owner, 2)
        owner_large = large if sum(offset) % 2 == 0 else jnp.logical_not(large)

        @pl.when(owner_large)
        def _():
            remote(
                half_v.at[pl.ds(2 * owner_column, 2)], rs_v.at[pl.ds(2 * slot, 2)],
                rs_send, rs_recv, (2 * owner + core, c),
            ).start()

        @pl.when(jnp.logical_not(owner_large))
        def _():
            remote(
                half_v.at[pl.ds(32 + owner_column, 1)], rs_v.at[pl.ds(slot, 1)],
                rs_send, rs_recv, (2 * owner + core, c),
            ).start()

    loads[4].wait()
    input_products(0)
    input_parities(0)
    input_output(0)

    def own_piece(at, count):
        dst = rs_v.at[pl.ds(0, count * (CHIPS - 1))]
        pltpu.make_async_copy(dst, dst, rs_recv).wait()
        total = half_v[pl.ds(at, count)].astype(F32)
        for slot in range(CHIPS - 1):
            total = total + rs_v[count * slot : count * slot + count].astype(F32)
        here = pl.ds(core * PIECES + at, count)
        gr_v[here] = total.astype(BF)
        for offset in FAR_FIRST:
            src = gr_v.at[here]
            remote(src, src, ag_send, ag_recv, (2 * chip_at(offset) + core, c)).start()
            remote(src, src, sib_send, sib_recv, (2 * chip_at(offset) + 1 - core, c)).start()
        remote(src, src, sib_send, sib_recv, sibling).start()

    @pl.when(large)
    def _():
        own_piece(large_at, 2)

    @pl.when(jnp.logical_not(large))
    def _():
        own_piece(small_at, 1)

    input_products(1)
    input_parities(1)
    input_output(1)

    def rest(count, sem):
        dst = gr_v.at[pl.ds(0, count)]
        pltpu.make_async_copy(dst, dst, sem).wait()

    @pl.when(large)
    def _():
        rest(PIECES - 2, ag_recv)

    @pl.when(jnp.logical_not(large))
    def _():
        rest(PIECES - 1, ag_recv)


    rest(PIECES, sib_recv)

    for copy in sent:
        copy.wait_send()

    @pl.when(paired)
    def _():
        for copy in pair_copies:
            copy.wait_send()

    exchange.wait_send()

    @pl.when(large)
    def _():
        rest(PIECES - 2, rs_send)
        rest(2 * (CHIPS - 1), ag_send)
        rest(2 * CHIPS, sib_send)

    @pl.when(jnp.logical_not(large))
    def _():
        rest(PIECES - 1, rs_send)
        rest(CHIPS - 1, ag_send)
        rest(CHIPS, sib_send)


def finish(ig_v, gr_v, ig_out, sp_out, te_out, wide_v, sem):
    scale = 1.0 / math.sqrt(128 * 16 * 128)
    stores = [pltpu.make_async_copy(ig_v, ig_out, sem.at[4])]
    stores[0].start()
    for k in range(4):
        pieces = gr_v[24 * k : 24 * k + 24].reshape(12, 2, 16, 128)
        for side in range(2):
            wide_v[12 * k : 12 * k + 12, :, 128 * side : 128 * side + 128] = (
                pieces[:, side].astype(F32) * scale
            )
        dst = te_out if k == 0 else sp_out.at[pl.ds(12 * k - 12, 12)]
        store = pltpu.make_async_copy(wide_v.at[pl.ds(12 * k, 12)], dst, sem.at[k])
        store.start()
        stores.append(store)
    for store in stores:
        store.wait()


def shards(inputs, saved, cotangent, spatial_w, temporal_w):
    vmem = pltpu.VMEM
    dma = pltpu.SemaphoreType.DMA
    input_grad, grads = pl.pallas_call(
        kernel,
        out_shape=(
            pltpu.VMEM((2, 64, 16, 128), BF),
            pltpu.VMEM((2 * PIECES, 16, 128), BF),
        ),
        in_specs=[pl.BlockSpec(memory_space=pl.ANY)] * 5,
        out_specs=(
            pl.BlockSpec(memory_space=pltpu.VMEM),
            pl.BlockSpec(memory_space=pltpu.VMEM),
        ),
        scratch_shapes=[
            vmem((2, 64, 16, 128), BF),
            vmem((2, 64, 16, 128), BF),
            vmem((3, 3, 64, 256), BF),
            vmem((3, 256, 256), BF),
            vmem((4, 64, 512), BF),
            vmem((2, 4, 64, 512), BF),
            vmem((4, 2048, 128), F32),
            vmem((2, 576, 512), BF),
            vmem((128, 512), BF),
            vmem((768, 512), F32),
            vmem((2, 256, 512), BF),
            vmem((9, 64, 512), F32),
            vmem((2, 4, 64, 256), BF),
            vmem((1024, 128), F32),
            vmem((24, 2, 16, 128), BF),
            vmem((24, 2, 16, 128), F32),
            vmem((24, 2, 16, 128), BF),
            vmem((PIECES, 16, 128), BF),
            vmem((2 * (CHIPS - 1), 16, 128), BF),
            dma((5,)),
            dma((6,)),
            dma((6,)),
            dma((10,)),
            dma((2,)),
            dma, dma,
            dma, dma,
            dma, dma,
            dma, dma,
            pltpu.SemaphoreType.REGULAR((ROUNDS,)),
        ],
        compiler_params=pltpu.CompilerParams(
            collective_id=0, has_side_effects=True, vmem_limit_bytes=56 * 1024 * 1024
        ),
        name="space_time_backward",
    )(inputs, saved, cotangent, spatial_w, temporal_w)
    input_grad = pltpu.with_memory_space_constraint(input_grad, pltpu.VMEM)
    grads = pltpu.with_memory_space_constraint(grads, pltpu.VMEM)
    input_grad, spatial, temporal = pl.pallas_call(
        finish,
        out_shape=(
            jax.ShapeDtypeStruct((2, 64, 16, 128), BF),
            jax.ShapeDtypeStruct((36, 16, 256), F32),
            jax.ShapeDtypeStruct((12, 16, 256), F32),
        ),
        in_specs=[pl.BlockSpec(memory_space=pltpu.VMEM)] * 2,
        out_specs=[pl.BlockSpec(memory_space=pl.ANY)] * 3,
        scratch_shapes=[
            vmem((48, 16, 256), F32),
            dma((5,)),
        ],
        name="scale_gradients",
    )(input_grad, grads)
    return (input_grad, spatial.reshape(3, 3, 64, 256), temporal.reshape(3, 64, 256))


def solution(mesh):
    return jax.shard_map(
        shards,
        mesh=mesh,
        in_specs=(
            P("frames", "chan", None, None),
            P("frames", "chan", None, None),
            P("frames", "chan", None),
            P(None, None, "chan", None),
            P(),
        ),
        out_specs=(
            P("frames", "chan", None, None),
            P(None, None, "chan", None),
            P(None, "chan", None),
        ),
        check_vma=False,
    )
```

```python
import math

import jax
import jax.numpy as jnp
from jax import lax
from jax.experimental import pallas as pl
from jax.experimental.pallas import tpu as pltpu
from jax.sharding import PartitionSpec as P

BF = jnp.bfloat16
F32 = jnp.float32
CHIPS = 32
PIECES = 48


FAR_FIRST = sorted(
    [(i, j, k) for i in range(4) for j in range(4) for k in range(2) if i or j or k],
    key=lambda s: -(min(s[0], 4 - s[0]) + min(s[1], 4 - s[1]) + s[2]),
)


NEXT = [(1, 0, 0), (3, 0, 0), (0, 1, 0), (0, 3, 0), (0, 0, 1)]
ROUNDS = 4


def dot(a, b):
    return jnp.dot(a, b, preferred_element_type=F32)


def dot_nt(a, b):
    return lax.dot_general(a, b, (((1,), (1,)), ((), ())), preferred_element_type=F32)


def kernel(
    x_h, s_h, c_h, sw_h, tw_h,
    ig_v, gr_v,
    x_v, s_v, sw_v, tw_v, ring, halo, pool, q_v, sq_v, a_v, g_v, p_v, xe_v, z_v,
    given, kept, xch, half_v, rs_v,
    load_sem, ring_send_sem, ring_recv, fwd_send, halo_recv,
    xch_send, xch_recv, rs_send, rs_recv, ag_send, ag_recv, news,
):
    p = lax.axis_index("frames")
    c = lax.axis_index("chan")
    core = lax.rem(p, 2)
    chip = lax.div(p, 2)
    zl = lax.rem(chip, 2)
    column = lax.div(chip, 2)
    z = 2 * c + zl

    def in_ring(step):
        zz = lax.rem(z + step + 8, 8)
        return (4 * column + 2 * lax.rem(zz, 2) + core, lax.div(zz, 2))

    pair = p + 2 * core - 1
    paired = jnp.logical_and(pair >= 0, pair < 64)

    def in_pair(step):
        zz = lax.rem(z + step + 8, 8)
        return (4 * lax.div(pair, 4) + 2 * lax.rem(zz, 2) + 1 - core, lax.div(zz, 2))

    sibling = (p + 1 - 2 * core, c)

    barrier = pltpu.get_barrier_semaphore()

    def greet(device):
        pl.semaphore_signal(barrier, inc=1, device_id=device, device_id_type=pl.DeviceIdType.MESH)

    greet(in_ring(2))
    greet(in_ring(-2))
    greet(sibling)

    @pl.when(paired)
    def _():
        greet(in_pair(1))
        greet(in_pair(-1))

    x, y = lax.div(chip, 8), lax.rem(column, 4)

    def chip_at(offset):
        return 8 * lax.rem(x + offset[0], 4) + 2 * lax.rem(y + offset[1], 4) + lax.rem(zl + offset[2], 2)

    for offset in NEXT:
        greet((2 * chip_at(offset) + core, c))

    loads = [
        pltpu.make_async_copy(c_h.at[0], ring.at[c], load_sem.at[0]),
        pltpu.make_async_copy(s_h, s_v, load_sem.at[1]),
        pltpu.make_async_copy(x_h, x_v, load_sem.at[2]),
        pltpu.make_async_copy(tw_h, tw_v, load_sem.at[3]),
        pltpu.make_async_copy(sw_h, sw_v, load_sem.at[4]),
    ]
    for load in loads:
        load.start()

    pl.semaphore_wait(barrier, 3 + len(NEXT) + jnp.where(paired, 2, 0))
    loads[0].wait()

    def remote(src, dst, send, recv, device):
        return pltpu.make_async_remote_copy(
            src_ref=src, dst_ref=dst, send_sem=send, recv_sem=recv,
            device_id=device, device_id_type=pl.DeviceIdType.MESH,
        )

    sent = []

    def rows(half):
        return pl.ds(32 * half, 32)

    quarters = {step: lax.rem(c + step + 4, 4) for step in (-1, 0, 1, 2)}

    def ring_send(hop, quarter, half, index, src=None):
        copy = remote(
            ring.at[quarter, rows(half)] if src is None else src, ring.at[quarter, rows(half)],
            ring_send_sem.at[index], ring_recv.at[index], in_ring(hop),
        )
        copy.start()
        sent.append(copy)

    def ring_wait(quarter, half, index):
        dst = ring.at[quarter, rows(half)]
        remote(dst, dst, ring_send_sem.at[index], ring_recv.at[index], sibling).wait_recv()

    def to_sibling(src, quarter, index):
        copy = remote(src, halo.at[core, quarter], fwd_send.at[index], halo_recv.at[0], sibling)
        copy.start()
        sent.append(copy)

    pair_copies = []

    def to_pair(step, src, quarter, index, dst=None):
        copy = remote(
            src, halo.at[1 - core, quarter] if dst is None else dst,
            fwd_send.at[index], halo_recv.at[1], in_pair(step),
        )

        @pl.when(paired)
        def _():
            copy.start()

        pair_copies.append(copy)

    def to_pair_half(step, quarter, half, index):
        to_pair(
            step, ring.at[quarter, rows(half)], quarter, index,
            halo.at[1 - core, quarter, rows(half)],
        )

    for half in range(2):
        ring_send(2, c, half, half, ring.at[c, rows(half)])
        ring_send(-2, c, 1 - half, 3 - half, ring.at[c, rows(1 - half)])
    to_pair(1, ring.at[c], c, 4)
    to_pair(-1, ring.at[c], c, 5)
    to_sibling(ring.at[c], c, 0)

    def near_shards():
        below, above = quarters[-1], quarters[1]
        ring_wait(below, 0, 0)
        ring_send(2, below, 0, 4)
        ring_wait(above, 1, 3)
        ring_send(-2, above, 1, 5)
        to_pair_half(1, below, 0, 6)
        to_pair_half(-1, above, 1, 8)
        ring_wait(below, 1, 1)
        to_pair_half(1, below, 1, 7)
        ring_wait(above, 0, 2)
        to_pair_half(-1, above, 0, 9)
        to_sibling(ring.at[below], below, 1)
        to_sibling(ring.at[above], above, 2)

    def far_shard():
        ring_wait(quarters[2], 0, 4)
        ring_wait(quarters[2], 1, 5)
        to_sibling(ring.at[quarters[2]], quarters[2], 3)

    def spread_news(k):
        for offset in NEXT:
            pl.semaphore_signal(
                news.at[k], inc=1, device_id=(2 * chip_at(offset) + core, c),
                device_id_type=pl.DeviceIdType.MESH,
            )

    def hear_news(k):
        pl.semaphore_wait(news.at[k], len(NEXT))

    spread_news(0)

    lane = lax.broadcasted_iota(jnp.int32, (128, 384), 1)
    column_of = lax.broadcasted_iota(jnp.int32, (128, 384), 0)
    first = 2 * (lane & 63) + (lane >> 7) - 1
    pairs = jnp.where(
        jnp.logical_or(column_of == first, column_of == first + 1), 1.0, 0.0
    ).astype(BF)
    low = lax.broadcasted_iota(jnp.int32, (64, 128), 1) < 64

    loads[1].wait()
    for f in range(2):
        pool[0, pl.ds(f * 1024, 1024), :] = dot(
            s_v[f].reshape(1024, 128), pairs[:, 128:256]
        )
        height = [pool[0, pl.ds(f * 1024 + h, 64, stride=16), :] for h in range(16)]
        for j in range(4):
            upper = height[4 * j] + height[4 * j + 1]
            lower = height[4 * j + 2] + height[4 * j + 3]
            sq_v[pl.ds(64 * f, 64), 128 * j : 128 * j + 128] = jnp.where(low, upper, lower).astype(BF)

    loads[2].wait()
    for f in range(2):
        sums = dot(x_v[f].reshape(1024, 128), pairs)
        for b in range(3):
            pool[1 + b, pl.ds(f * 1024, 1024), :] = sums[:, 128 * b : 128 * b + 128]
    hear_news(0)
    spread_news(1)
    near_shards()
    hear_news(1)
    spread_news(2)
    for f in range(2):
        for b in range(3):
            height = [pool[1 + b, pl.ds(f * 1024 + h, 64, stride=16), :] for h in range(16)]
            total = (
                [height[0]] + [height[h] + height[h + 1] for h in range(15)] + [height[15]]
            )
            for a in range(3):
                for j in range(4):
                    q_v[f, pl.ds((3 * a + b) * 64, 64), 128 * j : 128 * j + 128] = jnp.where(
                        low, total[4 * j + a], total[4 * j + a + 2]
                    ).astype(BF)
    loads[3].wait()
    hear_news(2)
    spread_news(3)
    far_shard()

    own = ring[...].reshape(256, 512)
    a_v[...] = dot(tw_v[...].reshape(768, 256), own)
    t_own = dot_nt(sq_v[...], own)

    dst = halo.at[1 - core]
    pltpu.make_async_copy(dst, dst, halo_recv.at[0]).wait()

    @pl.when(paired)
    def _():
        dst = halo.at[core]
        pltpu.make_async_copy(dst, dst, halo_recv.at[1]).wait()

    @pl.when(jnp.logical_not(paired))
    def _():
        halo[core] = jnp.zeros((4, 64, 512), BF)

    before = halo[0].reshape(256, 512)
    after = halo[1].reshape(256, 512)
    middle = a_v[256:512]
    g_v[0] = ((a_v[0:256] + middle + dot(tw_v[2], before)) * 0.125).astype(BF)
    g_v[1] = ((dot(tw_v[0], after) + middle + a_v[512:768]) * 0.125).astype(BF)

    def put(dst, at, value):
        count = value.shape[0] // 16
        for side in range(2):
            piece = value[:, 128 * side : 128 * side + 128].reshape(count, 16, 128)
            dst[at : at + count, side] = piece.astype(dst.dtype)

    def spatial(dst, at, first_tap, last_tap):
        taps = slice(64 * first_tap, 64 * last_tap)
        put(dst, at, dot_nt(q_v[0, taps], g_v[0]) + dot_nt(q_v[1, taps], g_v[1]))

    def lower_half(dst):
        t_after = dot_nt(sq_v[64:128], after)
        t_before = dot_nt(sq_v[0:64], before)
        put(dst, 0, (t_own[0:64] + t_after) * 0.125)
        put(dst, 4, (t_own[0:64] + t_own[64:128]) * 0.125)
        put(dst, 8, (t_own[64:128] + t_before) * 0.125)
        spatial(dst, 12, 0, 3)

    def upper_half(dst):
        spatial(dst, 0, 3, 9)

    exchange = remote(given, xch, xch_send, xch_recv, sibling)

    @pl.when(core == 0)
    def _():
        upper_half(given)
        exchange.start()
        lower_half(kept)

    @pl.when(core == 1)
    def _():
        lower_half(given)
        exchange.start()
        upper_half(kept)

    def input_products(f):
        p_v[...] = dot(sw_v[...].reshape(576, 256), g_v[f]).reshape(9, 64, 512)

    cell = lax.broadcasted_iota(jnp.int32, (16, 512), 1)

    def input_parities(f):
        def tile(i, carry):
            here = pl.ds(pl.multiple_of(16 * i, 16), 16)
            tops, bottoms = [], []
            for b in range(3):
                t0, t1, t2 = p_v[b, here, :], p_v[3 + b, here, :], p_v[6 + b, here, :]
                tops.append(t0 + t1 + jnp.where(cell >= 64, pltpu.roll(t2, 64, 1), 0.0))
                bottoms.append(t1 + t2 + jnp.where(cell < 448, pltpu.roll(t0, 448, 1), 0.0))
            for r, (u0, u1, u2) in enumerate((tops, bottoms)):
                even = u0 + u1 + jnp.where((cell & 63) != 0, pltpu.roll(u2, 1, 1), 0.0)
                odd = u1 + u2 + jnp.where((cell & 63) != 63, pltpu.roll(u0, 511, 1), 0.0)
                for j in range(4):
                    cut = slice(128 * j, 128 * j + 128)
                    xe_v[r, j, here, 0:128] = even[:, cut].astype(BF)
                    xe_v[r, j, here, 128:256] = odd[:, cut].astype(BF)
            return carry

        lax.fori_loop(0, 4, tile, 0)

    k_of = lax.broadcasted_iota(jnp.int32, (256, 256), 0)
    w_of = lax.broadcasted_iota(jnp.int32, (256, 256), 1)
    place = ((k_of >> 6) & 1) * 128 + 2 * (k_of & 63) + (k_of >> 7)
    weave = jnp.where(w_of == place, 1.0, 0.0).astype(BF)

    def input_output(f):
        woven = dot(xe_v[...].reshape(512, 256), weave).reshape(2, 4, 64, 256)
        for r in range(2):
            for j in range(4):
                for k in range(2):
                    h = 2 * (2 * j + k) + r
                    z_v[pl.ds(h, 64, stride=16), :] = woven[r, j, :, 128 * k : 128 * k + 128]
        ig_v[f] = z_v[...].reshape(64, 16, 128).astype(BF)

    exchange.wait_recv()
    half_v[...] = (kept[...] + xch[...].astype(F32)).astype(BF).reshape(PIECES, 16, 128)
    hear_news(3)

    large = lax.rem(x + y + zl + core, 2) == 0
    large_at, small_at = 2 * column, 32 + column

    for slot, offset in enumerate(FAR_FIRST):
        owner = chip_at(offset)
        owner_column = lax.div(owner, 2)
        owner_large = large if sum(offset) % 2 == 0 else jnp.logical_not(large)

        @pl.when(owner_large)
        def _():
            remote(
                half_v.at[pl.ds(2 * owner_column, 2)], rs_v.at[pl.ds(2 * slot, 2)],
                rs_send, rs_recv, (2 * owner + core, c),
            ).start()

        @pl.when(jnp.logical_not(owner_large))
        def _():
            remote(
                half_v.at[pl.ds(32 + owner_column, 1)], rs_v.at[pl.ds(slot, 1)],
                rs_send, rs_recv, (2 * owner + core, c),
            ).start()

    loads[4].wait()
    input_products(0)
    input_parities(0)
    input_output(0)

    def own_piece(at, count):
        dst = rs_v.at[pl.ds(0, count * (CHIPS - 1))]
        pltpu.make_async_copy(dst, dst, rs_recv).wait()
        total = half_v[pl.ds(at, count)].astype(F32)
        for slot in range(CHIPS - 1):
            total = total + rs_v[count * slot : count * slot + count].astype(F32)
        here = pl.ds(core * PIECES + at, count)
        gr_v[here] = total.astype(BF)
        src = gr_v.at[here]

        def hand_out(target):
            for side in (1, 0):
                remote(src, src, ag_send.at[side], ag_recv.at[core], (2 * target + side, c)).start()

        remote(src, src, ag_send.at[1 - core], ag_recv.at[core], sibling).start()

        for i, j, k in [(0, 0, 0)] + FAR_FIRST[::-1]:
            target = 8 * i + 2 * j + k

            @pl.when(target != chip)
            def _():
                hand_out(target)


    @pl.when(large)
    def _():
        own_piece(large_at, 2)

    @pl.when(jnp.logical_not(large))
    def _():
        own_piece(small_at, 1)

    input_products(1)
    input_parities(1)
    input_output(1)

    def rest(count, sem):
        dst = gr_v.at[pl.ds(0, count)]
        pltpu.make_async_copy(dst, dst, sem).wait()

    @pl.when(large)
    def _():
        rest(PIECES - 2, ag_recv.at[core])

    @pl.when(jnp.logical_not(large))
    def _():
        rest(PIECES - 1, ag_recv.at[core])


    rest(PIECES, ag_recv.at[1 - core])

    for copy in sent:
        copy.wait_send()

    @pl.when(paired)
    def _():
        for copy in pair_copies:
            copy.wait_send()

    exchange.wait_send()

    @pl.when(large)
    def _():
        rest(PIECES - 2, rs_send)
        rest(2 * (CHIPS - 1), ag_send.at[core])
        rest(2 * CHIPS, ag_send.at[1 - core])

    @pl.when(jnp.logical_not(large))
    def _():
        rest(PIECES - 1, rs_send)
        rest(CHIPS - 1, ag_send.at[core])
        rest(CHIPS, ag_send.at[1 - core])


def finish(ig_v, gr_v, ig_out, sp_out, te_out, wide_v, sem):
    scale = 1.0 / math.sqrt(128 * 16 * 128)
    stores = [pltpu.make_async_copy(ig_v, ig_out, sem.at[4])]
    stores[0].start()
    for k in range(4):
        pieces = gr_v[24 * k : 24 * k + 24].reshape(12, 2, 16, 128)
        for side in range(2):
            wide_v[12 * k : 12 * k + 12, :, 128 * side : 128 * side + 128] = (
                pieces[:, side].astype(F32) * scale
            )
        dst = te_out if k == 0 else sp_out.at[pl.ds(12 * k - 12, 12)]
        store = pltpu.make_async_copy(wide_v.at[pl.ds(12 * k, 12)], dst, sem.at[k])
        store.start()
        stores.append(store)
    for store in stores:
        store.wait()


def shards(inputs, saved, cotangent, spatial_w, temporal_w):
    vmem = pltpu.VMEM
    dma = pltpu.SemaphoreType.DMA
    input_grad, grads = pl.pallas_call(
        kernel,
        out_shape=(
            pltpu.VMEM((2, 64, 16, 128), BF),
            pltpu.VMEM((2 * PIECES, 16, 128), BF),
        ),
        in_specs=[pl.BlockSpec(memory_space=pl.ANY)] * 5,
        out_specs=(
            pl.BlockSpec(memory_space=pltpu.VMEM),
            pl.BlockSpec(memory_space=pltpu.VMEM),
        ),
        scratch_shapes=[
            vmem((2, 64, 16, 128), BF),
            vmem((2, 64, 16, 128), BF),
            vmem((3, 3, 64, 256), BF),
            vmem((3, 256, 256), BF),
            vmem((4, 64, 512), BF),
            vmem((2, 4, 64, 512), BF),
            vmem((4, 2048, 128), F32),
            vmem((2, 576, 512), BF),
            vmem((128, 512), BF),
            vmem((768, 512), F32),
            vmem((2, 256, 512), BF),
            vmem((9, 64, 512), F32),
            vmem((2, 4, 64, 256), BF),
            vmem((1024, 128), F32),
            vmem((24, 2, 16, 128), BF),
            vmem((24, 2, 16, 128), F32),
            vmem((24, 2, 16, 128), BF),
            vmem((PIECES, 16, 128), BF),
            vmem((2 * (CHIPS - 1), 16, 128), BF),
            dma((5,)),
            dma((6,)),
            dma((6,)),
            dma((10,)),
            dma((2,)),
            dma, dma,
            dma, dma,
            dma((2,)), dma((2,)),
            pltpu.SemaphoreType.REGULAR((ROUNDS,)),
        ],
        compiler_params=pltpu.CompilerParams(
            collective_id=0, has_side_effects=True, vmem_limit_bytes=56 * 1024 * 1024
        ),
        name="space_time_backward",
    )(inputs, saved, cotangent, spatial_w, temporal_w)
    input_grad = pltpu.with_memory_space_constraint(input_grad, pltpu.VMEM)
    grads = pltpu.with_memory_space_constraint(grads, pltpu.VMEM)
    input_grad, spatial, temporal = pl.pallas_call(
        finish,
        out_shape=(
            jax.ShapeDtypeStruct((2, 64, 16, 128), BF),
            jax.ShapeDtypeStruct((36, 16, 256), F32),
            jax.ShapeDtypeStruct((12, 16, 256), F32),
        ),
        in_specs=[pl.BlockSpec(memory_space=pltpu.VMEM)] * 2,
        out_specs=[pl.BlockSpec(memory_space=pl.ANY)] * 3,
        scratch_shapes=[
            vmem((48, 16, 256), F32),
            dma((5,)),
        ],
        name="scale_gradients",
    )(input_grad, grads)
    return (input_grad, spatial.reshape(3, 3, 64, 256), temporal.reshape(3, 64, 256))


def solution(mesh):
    return jax.shard_map(
        shards,
        mesh=mesh,
        in_specs=(
            P("frames", "chan", None, None),
            P("frames", "chan", None, None),
            P("frames", "chan", None),
            P(None, None, "chan", None),
            P(),
        ),
        out_specs=(
            P("frames", "chan", None, None),
            P(None, None, "chan", None),
            P(None, "chan", None),
        ),
        check_vma=False,
    )
```

```python
import math

import jax
import jax.numpy as jnp
from jax import lax
from jax.experimental import pallas as pl
from jax.experimental.pallas import tpu as pltpu
from jax.sharding import PartitionSpec as P

BF = jnp.bfloat16
F32 = jnp.float32
CHIPS = 32
PARTS = 2
PIECES = 48


FAR_FIRST = sorted(
    [(i, j, k) for i in range(4) for j in range(4) for k in range(2) if i or j or k],
    key=lambda s: -(min(s[0], 4 - s[0]) + min(s[1], 4 - s[1]) + s[2]),
)


NEXT = [(1, 0, 0), (3, 0, 0), (0, 1, 0), (0, 3, 0), (0, 0, 1)]
ROUNDS = 4


def dot(a, b):
    return jnp.dot(a, b, preferred_element_type=F32)


def dot_nt(a, b):
    return lax.dot_general(a, b, (((1,), (1,)), ((), ())), preferred_element_type=F32)


def kernel(
    x_h, s_h, c_h, sw_h, tw_h,
    ig_v, gr_v,
    x_v, s_v, sw_v, tw_v, ring, halo, pool, q_v, sq_v, a_v, g_v, p_v, xe_v, z_v,
    given, kept, xch, half_v, rs_v,
    load_sem, ring_send_sem, ring_recv, fwd_send, halo_recv,
    xch_send, xch_recv, rs_send, rs_recv, ag_send, ag_recv, news,
):
    p = lax.axis_index("frames")
    c = lax.axis_index("chan")
    core = lax.rem(p, 2)
    chip = lax.div(p, 2)
    zl = lax.rem(chip, 2)
    column = lax.div(chip, 2)
    z = 2 * c + zl

    def in_ring(step):
        zz = lax.rem(z + step + 8, 8)
        return (4 * column + 2 * lax.rem(zz, 2) + core, lax.div(zz, 2))

    pair = p + 2 * core - 1
    paired = jnp.logical_and(pair >= 0, pair < 64)

    def in_pair(step):
        zz = lax.rem(z + step + 8, 8)
        return (4 * lax.div(pair, 4) + 2 * lax.rem(zz, 2) + 1 - core, lax.div(zz, 2))

    sibling = (p + 1 - 2 * core, c)

    barrier = pltpu.get_barrier_semaphore()

    def greet(device):
        pl.semaphore_signal(barrier, inc=1, device_id=device, device_id_type=pl.DeviceIdType.MESH)

    greet(in_ring(2))
    greet(in_ring(-2))
    greet(sibling)

    @pl.when(paired)
    def _():
        greet(in_pair(1))
        greet(in_pair(-1))

    x, y = lax.div(chip, 8), lax.rem(column, 4)

    def chip_at(offset):
        return 8 * lax.rem(x + offset[0], 4) + 2 * lax.rem(y + offset[1], 4) + lax.rem(zl + offset[2], 2)

    for offset in NEXT:
        greet((2 * chip_at(offset) + core, c))

    loads = [
        pltpu.make_async_copy(c_h.at[0], ring.at[c], load_sem.at[0]),
        pltpu.make_async_copy(s_h, s_v, load_sem.at[1]),
        pltpu.make_async_copy(x_h, x_v, load_sem.at[2]),
        pltpu.make_async_copy(tw_h, tw_v, load_sem.at[3]),
        pltpu.make_async_copy(sw_h, sw_v, load_sem.at[4]),
    ]
    for load in loads:
        load.start()

    pl.semaphore_wait(barrier, 3 + len(NEXT) + jnp.where(paired, 2, 0))
    loads[0].wait()

    def remote(src, dst, send, recv, device):
        return pltpu.make_async_remote_copy(
            src_ref=src, dst_ref=dst, send_sem=send, recv_sem=recv,
            device_id=device, device_id_type=pl.DeviceIdType.MESH,
        )

    sent = []

    def rows(part):
        return pl.ds(64 // PARTS * part, 64 // PARTS)

    quarters = {step: lax.rem(c + step + 4, 4) for step in (-1, 0, 1, 2)}

    def ring_send(hop, quarter, part, index, src=None):
        copy = remote(
            ring.at[quarter, rows(part)] if src is None else src, ring.at[quarter, rows(part)],
            ring_send_sem.at[index], ring_recv.at[index], in_ring(hop),
        )
        copy.start()
        sent.append(copy)

    def ring_wait(quarter, part, index):
        dst = ring.at[quarter, rows(part)]
        remote(dst, dst, ring_send_sem.at[index], ring_recv.at[index], sibling).wait_recv()

    def to_sibling(src, quarter, index):
        copy = remote(src, halo.at[core, quarter], fwd_send.at[index], halo_recv.at[0], sibling)
        copy.start()
        sent.append(copy)

    pair_copies = []

    def to_pair(step, src, quarter, index, dst=None):
        copy = remote(
            src, halo.at[1 - core, quarter] if dst is None else dst,
            fwd_send.at[index], halo_recv.at[1], in_pair(step),
        )

        @pl.when(paired)
        def _():
            copy.start()

        pair_copies.append(copy)

    def to_pair_part(step, quarter, part, index):
        to_pair(
            step, ring.at[quarter, rows(part)], quarter, index,
            halo.at[1 - core, quarter, rows(part)],
        )

    for part in range(PARTS):
        ring_send(2, c, part, part, ring.at[c, rows(part)])
        ring_send(-2, c, PARTS - 1 - part, 2 * PARTS - 1 - part, ring.at[c, rows(PARTS - 1 - part)])
    to_pair(1, ring.at[c], c, 4)
    to_pair(-1, ring.at[c], c, 5)
    to_sibling(ring.at[c], c, 0)

    def near_shards():
        below, above = quarters[-1], quarters[1]
        for part in range(PARTS):
            last = PARTS - 1 - part
            ring_wait(below, part, part)
            if part < PARTS // 2:
                ring_send(2, below, part, 2 * PARTS + part)
            ring_wait(above, last, PARTS + last)
            if part < PARTS // 2:
                ring_send(-2, above, last, 2 * PARTS + last)
            to_pair_part(1, below, part, 6 + part)
            to_pair_part(-1, above, last, 6 + PARTS + last)
        to_sibling(ring.at[below], below, 1)
        to_sibling(ring.at[above], above, 2)

    def far_shard():
        for part in range(PARTS):
            ring_wait(quarters[2], part, 2 * PARTS + part)
        to_sibling(ring.at[quarters[2]], quarters[2], 3)

    def spread_news(k):
        for offset in NEXT:
            pl.semaphore_signal(
                news.at[k], inc=1, device_id=(2 * chip_at(offset) + core, c),
                device_id_type=pl.DeviceIdType.MESH,
            )

    def hear_news(k):
        pl.semaphore_wait(news.at[k], len(NEXT))

    spread_news(0)

    lane = lax.broadcasted_iota(jnp.int32, (128, 384), 1)
    column_of = lax.broadcasted_iota(jnp.int32, (128, 384), 0)
    first = 2 * (lane & 63) + (lane >> 7) - 1
    pairs = jnp.where(
        jnp.logical_or(column_of == first, column_of == first + 1), 1.0, 0.0
    ).astype(BF)
    low = lax.broadcasted_iota(jnp.int32, (64, 128), 1) < 64

    loads[1].wait()
    for f in range(2):
        pool[0, pl.ds(f * 1024, 1024), :] = dot(
            s_v[f].reshape(1024, 128), pairs[:, 128:256]
        )
        height = [pool[0, pl.ds(f * 1024 + h, 64, stride=16), :] for h in range(16)]
        for j in range(4):
            upper = height[4 * j] + height[4 * j + 1]
            lower = height[4 * j + 2] + height[4 * j + 3]
            sq_v[pl.ds(64 * f, 64), 128 * j : 128 * j + 128] = jnp.where(low, upper, lower).astype(BF)

    loads[2].wait()
    for f in range(2):
        sums = dot(x_v[f].reshape(1024, 128), pairs)
        for b in range(3):
            pool[1 + b, pl.ds(f * 1024, 1024), :] = sums[:, 128 * b : 128 * b + 128]
    hear_news(0)
    spread_news(1)
    near_shards()
    hear_news(1)
    spread_news(2)
    for f in range(2):
        for b in range(3):
            height = [pool[1 + b, pl.ds(f * 1024 + h, 64, stride=16), :] for h in range(16)]
            total = (
                [height[0]] + [height[h] + height[h + 1] for h in range(15)] + [height[15]]
            )
            for a in range(3):
                for j in range(4):
                    q_v[f, pl.ds((3 * a + b) * 64, 64), 128 * j : 128 * j + 128] = jnp.where(
                        low, total[4 * j + a], total[4 * j + a + 2]
                    ).astype(BF)
    loads[3].wait()
    hear_news(2)
    spread_news(3)
    far_shard()

    own = ring[...].reshape(256, 512)
    taps = dot(tw_v[...].reshape(768, 256), own)
    a_v[0] = taps[0:256] + taps[256:512]
    a_v[1] = taps[256:512] + taps[512:768]
    t_own = dot_nt(sq_v[...], own)

    dst = halo.at[1 - core]
    pltpu.make_async_copy(dst, dst, halo_recv.at[0]).wait()

    @pl.when(paired)
    def _():
        dst = halo.at[core]
        pltpu.make_async_copy(dst, dst, halo_recv.at[1]).wait()

    @pl.when(jnp.logical_not(paired))
    def _():
        halo[core] = jnp.zeros((4, 64, 512), BF)

    before = halo[0].reshape(256, 512)
    after = halo[1].reshape(256, 512)
    g_v[0] = ((a_v[0] + dot(tw_v[2], before)) * 0.125).astype(BF)
    g_v[1] = ((a_v[1] + dot(tw_v[0], after)) * 0.125).astype(BF)

    def put(dst, at, value):
        count = value.shape[0] // 16
        for side in range(2):
            piece = value[:, 128 * side : 128 * side + 128].reshape(count, 16, 128)
            dst[at : at + count, side] = piece.astype(dst.dtype)

    def spatial(dst, at, first_tap, last_tap):
        taps = slice(64 * first_tap, 64 * last_tap)
        put(dst, at, dot_nt(q_v[0, taps], g_v[0]) + dot_nt(q_v[1, taps], g_v[1]))

    def lower_half(dst):
        t_after = dot_nt(sq_v[64:128], after)
        t_before = dot_nt(sq_v[0:64], before)
        put(dst, 0, (t_own[0:64] + t_after) * 0.125)
        put(dst, 4, (t_own[0:64] + t_own[64:128]) * 0.125)
        put(dst, 8, (t_own[64:128] + t_before) * 0.125)
        spatial(dst, 12, 0, 3)

    def upper_half(dst):
        spatial(dst, 0, 3, 9)

    exchange = remote(given, xch, xch_send, xch_recv, sibling)

    @pl.when(core == 0)
    def _():
        upper_half(given)
        exchange.start()
        lower_half(kept)

    @pl.when(core == 1)
    def _():
        lower_half(given)
        exchange.start()
        upper_half(kept)

    def input_products(f):
        p_v[...] = dot(sw_v[...].reshape(576, 256), g_v[f]).reshape(9, 64, 512)

    cell = lax.broadcasted_iota(jnp.int32, (16, 512), 1)

    def input_parities(f):
        def tile(i, carry):
            here = pl.ds(pl.multiple_of(16 * i, 16), 16)
            tops, bottoms = [], []
            for b in range(3):
                t0, t1, t2 = p_v[b, here, :], p_v[3 + b, here, :], p_v[6 + b, here, :]
                tops.append(t0 + t1 + jnp.where(cell >= 64, pltpu.roll(t2, 64, 1), 0.0))
                bottoms.append(t1 + t2 + jnp.where(cell < 448, pltpu.roll(t0, 448, 1), 0.0))
            for r, (u0, u1, u2) in enumerate((tops, bottoms)):
                even = u0 + u1 + jnp.where((cell & 63) != 0, pltpu.roll(u2, 1, 1), 0.0)
                odd = u1 + u2 + jnp.where((cell & 63) != 63, pltpu.roll(u0, 511, 1), 0.0)
                for j in range(4):
                    cut = slice(128 * j, 128 * j + 128)
                    xe_v[r, j, here, 0:128] = even[:, cut].astype(BF)
                    xe_v[r, j, here, 128:256] = odd[:, cut].astype(BF)
            return carry

        lax.fori_loop(0, 4, tile, 0)

    k_of = lax.broadcasted_iota(jnp.int32, (256, 256), 0)
    w_of = lax.broadcasted_iota(jnp.int32, (256, 256), 1)
    place = ((k_of >> 6) & 1) * 128 + 2 * (k_of & 63) + (k_of >> 7)
    weave = jnp.where(w_of == place, 1.0, 0.0).astype(BF)

    def input_output(f):
        woven = dot(xe_v[...].reshape(512, 256), weave).reshape(2, 4, 64, 256)
        for r in range(2):
            for j in range(4):
                for k in range(2):
                    h = 2 * (2 * j + k) + r
                    z_v[pl.ds(h, 64, stride=16), :] = woven[r, j, :, 128 * k : 128 * k + 128]
        ig_v[f] = z_v[0:1024].reshape(64, 16, 128).astype(BF)

    exchange.wait_recv()
    half_v[...] = (kept[...] + xch[...].astype(F32)).astype(BF).reshape(PIECES, 16, 128)
    hear_news(3)

    large = lax.rem(x + y + zl + core, 2) == 0
    large_at, small_at = 2 * column, 32 + column

    for slot, offset in enumerate(FAR_FIRST):
        owner = chip_at(offset)
        owner_column = lax.div(owner, 2)
        owner_large = large if sum(offset) % 2 == 0 else jnp.logical_not(large)

        @pl.when(owner_large)
        def _():
            remote(
                half_v.at[pl.ds(2 * owner_column, 2)], rs_v.at[pl.ds(2 * slot, 2)],
                rs_send, rs_recv, (2 * owner + core, c),
            ).start()

        @pl.when(jnp.logical_not(owner_large))
        def _():
            remote(
                half_v.at[pl.ds(32 + owner_column, 1)], rs_v.at[pl.ds(slot, 1)],
                rs_send, rs_recv, (2 * owner + core, c),
            ).start()

    loads[4].wait()
    input_products(0)
    input_parities(0)
    input_output(0)

    def own_piece(at, count):
        dst = rs_v.at[pl.ds(0, count * (CHIPS - 1))]
        pltpu.make_async_copy(dst, dst, rs_recv).wait()
        total = half_v[pl.ds(at, count)].astype(F32)
        for slot in range(CHIPS - 1):
            total = total + rs_v[count * slot : count * slot + count].astype(F32)
        here = pl.ds(core * PIECES + at, count)
        gr_v[here] = total.astype(BF)
        src = gr_v.at[here]

        def hand_out(target):
            for side in (1, 0):
                remote(src, src, ag_send.at[side], ag_recv.at[core], (2 * target + side, c)).start()

        remote(src, src, ag_send.at[1 - core], ag_recv.at[core], sibling).start()

        for i, j, k in [(0, 0, 0)] + FAR_FIRST[::-1]:
            target = 8 * i + 2 * j + k

            @pl.when(target != chip)
            def _():
                hand_out(target)


    @pl.when(large)
    def _():
        own_piece(large_at, 2)

    @pl.when(jnp.logical_not(large))
    def _():
        own_piece(small_at, 1)

    input_products(1)
    input_parities(1)
    input_output(1)

    def rest(count, sem):
        dst = gr_v.at[pl.ds(0, count)]
        pltpu.make_async_copy(dst, dst, sem).wait()

    @pl.when(large)
    def _():
        rest(PIECES - 2, ag_recv.at[core])

    @pl.when(jnp.logical_not(large))
    def _():
        rest(PIECES - 1, ag_recv.at[core])


    rest(PIECES, ag_recv.at[1 - core])

    for copy in sent:
        copy.wait_send()

    @pl.when(paired)
    def _():
        for copy in pair_copies:
            copy.wait_send()

    exchange.wait_send()

    @pl.when(large)
    def _():
        rest(PIECES - 2, rs_send)
        rest(2 * (CHIPS - 1), ag_send.at[core])
        rest(2 * CHIPS, ag_send.at[1 - core])

    @pl.when(jnp.logical_not(large))
    def _():
        rest(PIECES - 1, rs_send)
        rest(CHIPS - 1, ag_send.at[core])
        rest(CHIPS, ag_send.at[1 - core])


def finish(ig_v, gr_v, ig_out, sp_out, te_out, wide_v, sem):
    scale = 1.0 / math.sqrt(128 * 16 * 128)
    stores = [pltpu.make_async_copy(ig_v, ig_out, sem.at[4])]
    stores[0].start()
    for k in range(4):
        pieces = gr_v[24 * k : 24 * k + 24].reshape(12, 2, 16, 128)
        for side in range(2):
            wide_v[12 * k : 12 * k + 12, :, 128 * side : 128 * side + 128] = (
                pieces[:, side].astype(F32) * scale
            )
        dst = te_out if k == 0 else sp_out.at[pl.ds(12 * k - 12, 12)]
        store = pltpu.make_async_copy(wide_v.at[pl.ds(12 * k, 12)], dst, sem.at[k])
        store.start()
        stores.append(store)
    for store in stores:
        store.wait()


def shards(inputs, saved, cotangent, spatial_w, temporal_w):
    vmem = pltpu.VMEM
    dma = pltpu.SemaphoreType.DMA
    input_grad, grads = pl.pallas_call(
        kernel,
        out_shape=(
            pltpu.VMEM((2, 64, 16, 128), BF),
            pltpu.VMEM((2 * PIECES, 16, 128), BF),
        ),
        in_specs=[pl.BlockSpec(memory_space=pl.ANY)] * 5,
        out_specs=(
            pl.BlockSpec(memory_space=pltpu.VMEM),
            pl.BlockSpec(memory_space=pltpu.VMEM),
        ),
        scratch_shapes=[
            vmem((2, 64, 16, 128), BF),
            vmem((2, 64, 16, 128), BF),
            vmem((3, 3, 64, 256), BF),
            vmem((3, 256, 256), BF),
            vmem((4, 64, 512), BF),
            vmem((2, 4, 64, 512), BF),
            vmem((4, 2048 + 16, 128), F32),
            vmem((2, 576, 512), BF),
            vmem((128, 512), BF),
            vmem((2, 256, 512), F32),
            vmem((2, 256, 512), BF),
            vmem((9, 64, 512), F32),
            vmem((2, 4, 64, 256), BF),
            vmem((1024 + 16, 128), F32),
            vmem((24, 2, 16, 128), BF),
            vmem((24, 2, 16, 128), F32),
            vmem((24, 2, 16, 128), BF),
            vmem((PIECES, 16, 128), BF),
            vmem((2 * (CHIPS - 1), 16, 128), BF),
            dma((5,)),
            dma((3 * PARTS,)),
            dma((3 * PARTS,)),
            dma((6 + 2 * PARTS,)),
            dma((2,)),
            dma, dma,
            dma, dma,
            dma((2,)), dma((2,)),
            pltpu.SemaphoreType.REGULAR((ROUNDS,)),
        ],
        compiler_params=pltpu.CompilerParams(
            collective_id=0, has_side_effects=True, vmem_limit_bytes=56 * 1024 * 1024
        ),
        name="space_time_backward",
    )(inputs, saved, cotangent, spatial_w, temporal_w)
    input_grad = pltpu.with_memory_space_constraint(input_grad, pltpu.VMEM)
    grads = pltpu.with_memory_space_constraint(grads, pltpu.VMEM)
    input_grad, spatial, temporal = pl.pallas_call(
        finish,
        out_shape=(
            jax.ShapeDtypeStruct((2, 64, 16, 128), BF),
            jax.ShapeDtypeStruct((36, 16, 256), F32),
            jax.ShapeDtypeStruct((12, 16, 256), F32),
        ),
        in_specs=[pl.BlockSpec(memory_space=pltpu.VMEM)] * 2,
        out_specs=[pl.BlockSpec(memory_space=pl.ANY)] * 3,
        scratch_shapes=[
            vmem((48, 16, 256), F32),
            dma((5,)),
        ],
        name="scale_gradients",
    )(input_grad, grads)
    return (input_grad, spatial.reshape(3, 3, 64, 256), temporal.reshape(3, 64, 256))


def solution(mesh):
    return jax.shard_map(
        shards,
        mesh=mesh,
        in_specs=(
            P("frames", "chan", None, None),
            P("frames", "chan", None, None),
            P("frames", "chan", None),
            P(None, None, "chan", None),
            P(),
        ),
        out_specs=(
            P("frames", "chan", None, None),
            P(None, None, "chan", None),
            P(None, "chan", None),
        ),
        check_vma=False,
    )
```

```python
import math

import jax
import jax.numpy as jnp
from jax import lax
from jax.experimental import pallas as pl
from jax.experimental.pallas import tpu as pltpu
from jax.sharding import PartitionSpec as P

BF = jnp.bfloat16
F32 = jnp.float32
CHIPS = 32
PARTS = 2
PIECES = 48


FAR_FIRST = sorted(
    [(i, j, k) for i in range(4) for j in range(4) for k in range(2) if i or j or k],
    key=lambda s: (-(min(s[0], 4 - s[0]) + min(s[1], 4 - s[1]) + s[2]), s[2], s[0] + s[1]),
)


NEXT = [(1, 0, 0), (3, 0, 0), (0, 1, 0), (0, 3, 0), (0, 0, 1)]
ROUNDS = 4


def dot(a, b):
    return jnp.dot(a, b, preferred_element_type=F32)


def dot_nt(a, b):
    return lax.dot_general(a, b, (((1,), (1,)), ((), ())), preferred_element_type=F32)


def kernel(
    x_h, s_h, c_h, sw_h, tw_h,
    ig_v, gr_v,
    x_v, s_v, sw_v, tw_v, ring, halo, pool, q_v, sq_v, a_v, g_v, p_v, xe_v, z_v,
    given, kept, xch, half_v, rs_v,
    load_sem, ring_send_sem, ring_recv, fwd_send, halo_recv,
    xch_send, xch_recv, rs_send, rs_recv, ag_send, ag_recv, news,
):
    p = lax.axis_index("frames")
    c = lax.axis_index("chan")
    core = lax.rem(p, 2)
    chip = lax.div(p, 2)
    zl = lax.rem(chip, 2)
    column = lax.div(chip, 2)
    z = 2 * c + zl

    def in_ring(step):
        zz = lax.rem(z + step + 8, 8)
        return (4 * column + 2 * lax.rem(zz, 2) + core, lax.div(zz, 2))

    pair = p + 2 * core - 1
    paired = jnp.logical_and(pair >= 0, pair < 64)

    def in_pair(step):
        zz = lax.rem(z + step + 8, 8)
        return (4 * lax.div(pair, 4) + 2 * lax.rem(zz, 2) + 1 - core, lax.div(zz, 2))

    sibling = (p + 1 - 2 * core, c)

    barrier = pltpu.get_barrier_semaphore()

    def greet(device):
        pl.semaphore_signal(barrier, inc=1, device_id=device, device_id_type=pl.DeviceIdType.MESH)

    greet(in_ring(2))
    greet(in_ring(-2))
    greet(sibling)

    @pl.when(paired)
    def _():
        greet(in_pair(1))
        greet(in_pair(-1))

    x, y = lax.div(chip, 8), lax.rem(column, 4)

    def chip_at(offset):
        return 8 * lax.rem(x + offset[0], 4) + 2 * lax.rem(y + offset[1], 4) + lax.rem(zl + offset[2], 2)

    for offset in NEXT:
        greet((2 * chip_at(offset) + core, c))

    loads = [
        pltpu.make_async_copy(c_h.at[0], ring.at[c], load_sem.at[0]),
        pltpu.make_async_copy(s_h, s_v, load_sem.at[1]),
        pltpu.make_async_copy(x_h, x_v, load_sem.at[2]),
        pltpu.make_async_copy(tw_h, tw_v, load_sem.at[3]),
        pltpu.make_async_copy(sw_h, sw_v, load_sem.at[4]),
    ]
    for load in loads:
        load.start()

    pl.semaphore_wait(barrier, 3 + len(NEXT) + jnp.where(paired, 2, 0))
    loads[0].wait()

    def remote(src, dst, send, recv, device):
        return pltpu.make_async_remote_copy(
            src_ref=src, dst_ref=dst, send_sem=send, recv_sem=recv,
            device_id=device, device_id_type=pl.DeviceIdType.MESH,
        )

    sent = []

    def rows(part):
        return pl.ds(64 // PARTS * part, 64 // PARTS)

    quarters = {step: lax.rem(c + step + 4, 4) for step in (-1, 0, 1, 2)}

    def ring_send(hop, quarter, part, index, src=None):
        copy = remote(
            ring.at[quarter, rows(part)] if src is None else src, ring.at[quarter, rows(part)],
            ring_send_sem.at[index], ring_recv.at[index], in_ring(hop),
        )
        copy.start()
        sent.append(copy)

    def ring_wait(quarter, part, index):
        dst = ring.at[quarter, rows(part)]
        remote(dst, dst, ring_send_sem.at[index], ring_recv.at[index], sibling).wait_recv()

    def to_sibling(src, quarter, index):
        copy = remote(src, halo.at[core, quarter], fwd_send.at[index], halo_recv.at[0], sibling)
        copy.start()
        sent.append(copy)

    pair_copies = []

    def to_pair(step, src, quarter, index, dst=None):
        copy = remote(
            src, halo.at[1 - core, quarter] if dst is None else dst,
            fwd_send.at[index], halo_recv.at[1], in_pair(step),
        )

        @pl.when(paired)
        def _():
            copy.start()

        pair_copies.append(copy)

    def to_pair_part(step, quarter, part, index):
        to_pair(
            step, ring.at[quarter, rows(part)], quarter, index,
            halo.at[1 - core, quarter, rows(part)],
        )

    for part in range(PARTS):
        ring_send(2, c, part, part, ring.at[c, rows(part)])
        ring_send(-2, c, PARTS - 1 - part, 2 * PARTS - 1 - part, ring.at[c, rows(PARTS - 1 - part)])
    to_pair(1, ring.at[c], c, 4)
    to_pair(-1, ring.at[c], c, 5)
    to_sibling(ring.at[c], c, 0)

    def near_shards():
        below, above = quarters[-1], quarters[1]
        for part in range(PARTS):
            last = PARTS - 1 - part
            ring_wait(below, part, part)
            if part < PARTS // 2:
                ring_send(2, below, part, 2 * PARTS + part)
            ring_wait(above, last, PARTS + last)
            if part < PARTS // 2:
                ring_send(-2, above, last, 2 * PARTS + last)
            to_pair_part(1, below, part, 6 + part)
            to_pair_part(-1, above, last, 6 + PARTS + last)
        to_sibling(ring.at[below], below, 1)
        to_sibling(ring.at[above], above, 2)

    def far_shard():
        for part in range(PARTS):
            ring_wait(quarters[2], part, 2 * PARTS + part)
        to_sibling(ring.at[quarters[2]], quarters[2], 3)

    def spread_news(k):
        for offset in NEXT:
            pl.semaphore_signal(
                news.at[k], inc=1, device_id=(2 * chip_at(offset) + core, c),
                device_id_type=pl.DeviceIdType.MESH,
            )

    def hear_news(k):
        pl.semaphore_wait(news.at[k], len(NEXT))

    spread_news(0)

    lane = lax.broadcasted_iota(jnp.int32, (128, 384), 1)
    column_of = lax.broadcasted_iota(jnp.int32, (128, 384), 0)
    first = 2 * (lane & 63) + (lane >> 7) - 1
    pairs = jnp.where(
        jnp.logical_or(column_of == first, column_of == first + 1), 1.0, 0.0
    ).astype(BF)
    low = lax.broadcasted_iota(jnp.int32, (64, 128), 1) < 64

    loads[1].wait()
    for f in range(2):
        pool[0, pl.ds(f * 1024, 1024), :] = dot(
            s_v[f].reshape(1024, 128), pairs[:, 128:256]
        )
        height = [pool[0, pl.ds(f * 1024 + h, 64, stride=16), :] for h in range(16)]
        for j in range(4):
            upper = height[4 * j] + height[4 * j + 1]
            lower = height[4 * j + 2] + height[4 * j + 3]
            sq_v[pl.ds(64 * f, 64), 128 * j : 128 * j + 128] = jnp.where(low, upper, lower).astype(BF)

    loads[2].wait()
    for f in range(2):
        sums = dot(x_v[f].reshape(1024, 128), pairs)
        for b in range(3):
            pool[1 + b, pl.ds(f * 1024, 1024), :] = sums[:, 128 * b : 128 * b + 128]
    hear_news(0)
    spread_news(1)
    near_shards()
    hear_news(1)
    spread_news(2)
    for f in range(2):
        for b in range(3):
            height = [pool[1 + b, pl.ds(f * 1024 + h, 64, stride=16), :] for h in range(16)]
            total = (
                [height[0]] + [height[h] + height[h + 1] for h in range(15)] + [height[15]]
            )
            for a in range(3):
                for j in range(4):
                    q_v[f, pl.ds((3 * a + b) * 64, 64), 128 * j : 128 * j + 128] = jnp.where(
                        low, total[4 * j + a], total[4 * j + a + 2]
                    ).astype(BF)
    loads[3].wait()
    hear_news(2)
    spread_news(3)
    far_shard()

    own = ring[...].reshape(256, 512)
    taps = dot(tw_v[...].reshape(768, 256), own)
    a_v[0] = taps[0:256] + taps[256:512]
    a_v[1] = taps[256:512] + taps[512:768]
    t_own = dot_nt(sq_v[...], own)

    dst = halo.at[1 - core]
    pltpu.make_async_copy(dst, dst, halo_recv.at[0]).wait()

    @pl.when(paired)
    def _():
        dst = halo.at[core]
        pltpu.make_async_copy(dst, dst, halo_recv.at[1]).wait()

    @pl.when(jnp.logical_not(paired))
    def _():
        halo[core] = jnp.zeros((4, 64, 512), BF)

    before = halo[0].reshape(256, 512)
    after = halo[1].reshape(256, 512)
    g_v[0] = ((a_v[0] + dot(tw_v[2], before)) * 0.125).astype(BF)
    g_v[1] = ((a_v[1] + dot(tw_v[0], after)) * 0.125).astype(BF)

    def put(dst, at, value):
        count = value.shape[0] // 16
        for side in range(2):
            piece = value[:, 128 * side : 128 * side + 128].reshape(count, 16, 128)
            dst[at : at + count, side] = piece.astype(dst.dtype)

    def spatial(dst, at, first_tap, last_tap):
        taps = slice(64 * first_tap, 64 * last_tap)
        put(dst, at, dot_nt(q_v[0, taps], g_v[0]) + dot_nt(q_v[1, taps], g_v[1]))

    def lower_half(dst):
        t_after = dot_nt(sq_v[64:128], after)
        t_before = dot_nt(sq_v[0:64], before)
        put(dst, 0, (t_own[0:64] + t_after) * 0.125)
        put(dst, 4, (t_own[0:64] + t_own[64:128]) * 0.125)
        put(dst, 8, (t_own[64:128] + t_before) * 0.125)
        spatial(dst, 12, 0, 3)

    def upper_half(dst):
        spatial(dst, 0, 3, 9)

    exchange = remote(given, xch, xch_send, xch_recv, sibling)

    @pl.when(core == 0)
    def _():
        upper_half(given)
        exchange.start()
        lower_half(kept)

    @pl.when(core == 1)
    def _():
        lower_half(given)
        exchange.start()
        upper_half(kept)

    def input_products(f):
        p_v[...] = dot(sw_v[...].reshape(576, 256), g_v[f]).reshape(9, 64, 512)

    cell = lax.broadcasted_iota(jnp.int32, (16, 512), 1)

    def input_parities(f):
        def tile(i, carry):
            here = pl.ds(pl.multiple_of(16 * i, 16), 16)
            tops, bottoms = [], []
            for b in range(3):
                t0, t1, t2 = p_v[b, here, :], p_v[3 + b, here, :], p_v[6 + b, here, :]
                tops.append(t0 + t1 + jnp.where(cell >= 64, pltpu.roll(t2, 64, 1), 0.0))
                bottoms.append(t1 + t2 + jnp.where(cell < 448, pltpu.roll(t0, 448, 1), 0.0))
            for r, (u0, u1, u2) in enumerate((tops, bottoms)):
                even = u0 + u1 + jnp.where((cell & 63) != 0, pltpu.roll(u2, 1, 1), 0.0)
                odd = u1 + u2 + jnp.where((cell & 63) != 63, pltpu.roll(u0, 511, 1), 0.0)
                for j in range(4):
                    cut = slice(128 * j, 128 * j + 128)
                    xe_v[r, j, here, 0:128] = even[:, cut].astype(BF)
                    xe_v[r, j, here, 128:256] = odd[:, cut].astype(BF)
            return carry

        lax.fori_loop(0, 4, tile, 0)

    k_of = lax.broadcasted_iota(jnp.int32, (256, 256), 0)
    w_of = lax.broadcasted_iota(jnp.int32, (256, 256), 1)
    place = ((k_of >> 6) & 1) * 128 + 2 * (k_of & 63) + (k_of >> 7)
    weave = jnp.where(w_of == place, 1.0, 0.0).astype(BF)

    def input_output(f):
        woven = dot(xe_v[...].reshape(512, 256), weave).reshape(2, 4, 64, 256)
        for r in range(2):
            for j in range(4):
                for k in range(2):
                    h = 2 * (2 * j + k) + r
                    z_v[pl.ds(h, 64, stride=16), :] = woven[r, j, :, 128 * k : 128 * k + 128]
        ig_v[f] = z_v[0:1024].reshape(64, 16, 128).astype(BF)

    exchange.wait_recv()
    half_v[...] = (kept[...] + xch[...].astype(F32)).astype(BF).reshape(PIECES, 16, 128)
    hear_news(3)

    large = lax.rem(x + y + zl + core, 2) == 0
    large_at, small_at = 2 * column, 32 + column

    for slot, offset in enumerate(FAR_FIRST):
        owner = chip_at(offset)
        owner_column = lax.div(owner, 2)
        owner_large = large if sum(offset) % 2 == 0 else jnp.logical_not(large)

        @pl.when(owner_large)
        def _():
            remote(
                half_v.at[pl.ds(2 * owner_column, 2)], rs_v.at[pl.ds(2 * slot, 2)],
                rs_send, rs_recv, (2 * owner + core, c),
            ).start()

        @pl.when(jnp.logical_not(owner_large))
        def _():
            remote(
                half_v.at[pl.ds(32 + owner_column, 1)], rs_v.at[pl.ds(slot, 1)],
                rs_send, rs_recv, (2 * owner + core, c),
            ).start()

    loads[4].wait()
    input_products(0)
    input_parities(0)
    input_output(0)

    def own_piece(at, count):
        dst = rs_v.at[pl.ds(0, count * (CHIPS - 1))]
        pltpu.make_async_copy(dst, dst, rs_recv).wait()
        total = half_v[pl.ds(at, count)].astype(F32)
        for slot in range(CHIPS - 1):
            total = total + rs_v[count * slot : count * slot + count].astype(F32)
        here = pl.ds(core * PIECES + at, count)
        gr_v[here] = total.astype(BF)
        src = gr_v.at[here]

        def hand_out(target):
            for side in (1, 0):
                remote(src, src, ag_send.at[side], ag_recv.at[core], (2 * target + side, c)).start()

        remote(src, src, ag_send.at[1 - core], ag_recv.at[core], sibling).start()

        for i, j, k in [(0, 0, 0)] + FAR_FIRST[::-1]:
            target = 8 * i + 2 * j + k

            @pl.when(target != chip)
            def _():
                hand_out(target)


    @pl.when(large)
    def _():
        own_piece(large_at, 2)

    @pl.when(jnp.logical_not(large))
    def _():
        own_piece(small_at, 1)

    input_products(1)
    input_parities(1)
    input_output(1)

    def rest(count, sem):
        dst = gr_v.at[pl.ds(0, count)]
        pltpu.make_async_copy(dst, dst, sem).wait()

    @pl.when(large)
    def _():
        rest(PIECES - 2, ag_recv.at[core])

    @pl.when(jnp.logical_not(large))
    def _():
        rest(PIECES - 1, ag_recv.at[core])


    rest(PIECES, ag_recv.at[1 - core])

    for copy in sent:
        copy.wait_send()

    @pl.when(paired)
    def _():
        for copy in pair_copies:
            copy.wait_send()

    exchange.wait_send()

    @pl.when(large)
    def _():
        rest(PIECES - 2, rs_send)
        rest(2 * (CHIPS - 1), ag_send.at[core])
        rest(2 * CHIPS, ag_send.at[1 - core])

    @pl.when(jnp.logical_not(large))
    def _():
        rest(PIECES - 1, rs_send)
        rest(CHIPS - 1, ag_send.at[core])
        rest(CHIPS, ag_send.at[1 - core])


def finish(ig_v, gr_v, ig_out, sp_out, te_out, wide_v, sem):
    scale = 1.0 / math.sqrt(128 * 16 * 128)
    stores = [pltpu.make_async_copy(ig_v, ig_out, sem.at[4])]
    stores[0].start()
    for k in range(4):
        pieces = gr_v[24 * k : 24 * k + 24].reshape(12, 2, 16, 128)
        for side in range(2):
            wide_v[12 * k : 12 * k + 12, :, 128 * side : 128 * side + 128] = (
                pieces[:, side].astype(F32) * scale
            )
        dst = te_out if k == 0 else sp_out.at[pl.ds(12 * k - 12, 12)]
        store = pltpu.make_async_copy(wide_v.at[pl.ds(12 * k, 12)], dst, sem.at[k])
        store.start()
        stores.append(store)
    for store in stores:
        store.wait()


def shards(inputs, saved, cotangent, spatial_w, temporal_w):
    vmem = pltpu.VMEM
    dma = pltpu.SemaphoreType.DMA
    input_grad, grads = pl.pallas_call(
        kernel,
        out_shape=(
            pltpu.VMEM((2, 64, 16, 128), BF),
            pltpu.VMEM((2 * PIECES, 16, 128), BF),
        ),
        in_specs=[pl.BlockSpec(memory_space=pl.ANY)] * 5,
        out_specs=(
            pl.BlockSpec(memory_space=pltpu.VMEM),
            pl.BlockSpec(memory_space=pltpu.VMEM),
        ),
        scratch_shapes=[
            vmem((2, 64, 16, 128), BF),
            vmem((2, 64, 16, 128), BF),
            vmem((3, 3, 64, 256), BF),
            vmem((3, 256, 256), BF),
            vmem((4, 64, 512), BF),
            vmem((2, 4, 64, 512), BF),
            vmem((4, 2048 + 16, 128), F32),
            vmem((2, 576, 512), BF),
            vmem((128, 512), BF),
            vmem((2, 256, 512), F32),
            vmem((2, 256, 512), BF),
            vmem((9, 64, 512), F32),
            vmem((2, 4, 64, 256), BF),
            vmem((1024 + 16, 128), F32),
            vmem((24, 2, 16, 128), BF),
            vmem((24, 2, 16, 128), F32),
            vmem((24, 2, 16, 128), BF),
            vmem((PIECES, 16, 128), BF),
            vmem((2 * (CHIPS - 1), 16, 128), BF),
            dma((5,)),
            dma((3 * PARTS,)),
            dma((3 * PARTS,)),
            dma((6 + 2 * PARTS,)),
            dma((2,)),
            dma, dma,
            dma, dma,
            dma((2,)), dma((2,)),
            pltpu.SemaphoreType.REGULAR((ROUNDS,)),
        ],
        compiler_params=pltpu.CompilerParams(
            collective_id=0, has_side_effects=True, vmem_limit_bytes=56 * 1024 * 1024
        ),
        name="space_time_backward",
    )(inputs, saved, cotangent, spatial_w, temporal_w)
    input_grad = pltpu.with_memory_space_constraint(input_grad, pltpu.VMEM)
    grads = pltpu.with_memory_space_constraint(grads, pltpu.VMEM)
    input_grad, spatial, temporal = pl.pallas_call(
        finish,
        out_shape=(
            jax.ShapeDtypeStruct((2, 64, 16, 128), BF),
            jax.ShapeDtypeStruct((36, 16, 256), F32),
            jax.ShapeDtypeStruct((12, 16, 256), F32),
        ),
        in_specs=[pl.BlockSpec(memory_space=pltpu.VMEM)] * 2,
        out_specs=[pl.BlockSpec(memory_space=pl.ANY)] * 3,
        scratch_shapes=[
            vmem((48, 16, 256), F32),
            dma((5,)),
        ],
        name="scale_gradients",
    )(input_grad, grads)
    return (input_grad, spatial.reshape(3, 3, 64, 256), temporal.reshape(3, 64, 256))


def solution(mesh):
    return jax.shard_map(
        shards,
        mesh=mesh,
        in_specs=(
            P("frames", "chan", None, None),
            P("frames", "chan", None, None),
            P("frames", "chan", None),
            P(None, None, "chan", None),
            P(),
        ),
        out_specs=(
            P("frames", "chan", None, None),
            P(None, None, "chan", None),
            P(None, "chan", None),
        ),
        check_vma=False,
    )
```

```python
import math

import jax
import jax.numpy as jnp
from jax import lax
from jax.experimental import pallas as pl
from jax.experimental.pallas import tpu as pltpu
from jax.sharding import PartitionSpec as P

BF = jnp.bfloat16
F32 = jnp.float32
CHIPS = 32
PARTS = 2
PIECES = 48


FAR_FIRST = sorted(
    [(i, j, k) for i in range(4) for j in range(4) for k in range(2) if i or j or k],
    key=lambda s: (-(min(s[0], 4 - s[0]) + min(s[1], 4 - s[1]) + s[2]), s[2], s[0] + s[1]),
)


NEXT = [(1, 0, 0), (3, 0, 0), (0, 1, 0), (0, 3, 0), (0, 0, 1)]
ROUNDS = 4


def dot(a, b):
    return jnp.dot(a, b, preferred_element_type=F32)


def dot_nt(a, b):
    return lax.dot_general(a, b, (((1,), (1,)), ((), ())), preferred_element_type=F32)


def kernel(
    x_h, s_h, c_h, sw_h, tw_h,
    ig_v, gr_v,
    x_v, s_v, sw_v, tw_v, ring, halo, pool, q_v, sq_v, a_v, g_v, p_v, xe_v, z_v,
    given, kept, xch, half_v, rs_v,
    load_sem, ring_send_sem, ring_recv, fwd_send, halo_recv,
    xch_send, xch_recv, rs_send, rs_recv, ag_send, ag_recv, news,
):
    p = lax.axis_index("frames")
    c = lax.axis_index("chan")
    core = lax.rem(p, 2)
    chip = lax.div(p, 2)
    zl = lax.rem(chip, 2)
    column = lax.div(chip, 2)
    z = 2 * c + zl

    def in_ring(step):
        zz = lax.rem(z + step + 8, 8)
        return (4 * column + 2 * lax.rem(zz, 2) + core, lax.div(zz, 2))

    pair = p + 2 * core - 1
    paired = jnp.logical_and(pair >= 0, pair < 64)

    def in_pair(step):
        zz = lax.rem(z + step + 8, 8)
        return (4 * lax.div(pair, 4) + 2 * lax.rem(zz, 2) + 1 - core, lax.div(zz, 2))

    sibling = (p + 1 - 2 * core, c)

    barrier = pltpu.get_barrier_semaphore()

    def greet(device):
        pl.semaphore_signal(barrier, inc=1, device_id=device, device_id_type=pl.DeviceIdType.MESH)

    greet(in_ring(2))
    greet(in_ring(-2))
    greet(sibling)

    @pl.when(paired)
    def _():
        greet(in_pair(1))
        greet(in_pair(-1))

    x, y = lax.div(chip, 8), lax.rem(column, 4)

    def chip_at(offset):
        return 8 * lax.rem(x + offset[0], 4) + 2 * lax.rem(y + offset[1], 4) + lax.rem(zl + offset[2], 2)

    for offset in NEXT:
        greet((2 * chip_at(offset) + core, c))

    loads = [
        pltpu.make_async_copy(c_h.at[0], ring.at[c], load_sem.at[0]),
        pltpu.make_async_copy(s_h, s_v, load_sem.at[1]),
        pltpu.make_async_copy(x_h, x_v, load_sem.at[2]),
        pltpu.make_async_copy(tw_h, tw_v, load_sem.at[3]),
        pltpu.make_async_copy(sw_h, sw_v, load_sem.at[4]),
    ]
    for load in loads:
        load.start()

    pl.semaphore_wait(barrier, 3 + len(NEXT) + jnp.where(paired, 2, 0))
    loads[0].wait()

    def remote(src, dst, send, recv, device):
        return pltpu.make_async_remote_copy(
            src_ref=src, dst_ref=dst, send_sem=send, recv_sem=recv,
            device_id=device, device_id_type=pl.DeviceIdType.MESH,
        )

    sent = []

    def rows(part):
        return pl.ds(64 // PARTS * part, 64 // PARTS)

    quarters = {step: lax.rem(c + step + 4, 4) for step in (-1, 0, 1, 2)}

    def ring_send(hop, quarter, part, index, src=None):
        copy = remote(
            ring.at[quarter, rows(part)] if src is None else src, ring.at[quarter, rows(part)],
            ring_send_sem.at[index], ring_recv.at[index], in_ring(hop),
        )
        copy.start()
        sent.append(copy)

    def ring_wait(quarter, part, index):
        dst = ring.at[quarter, rows(part)]
        remote(dst, dst, ring_send_sem.at[index], ring_recv.at[index], sibling).wait_recv()

    def to_sibling(src, quarter, index):
        copy = remote(src, halo.at[core, quarter], fwd_send.at[index], halo_recv.at[0], sibling)
        copy.start()
        sent.append(copy)

    pair_copies = []

    def to_pair(step, src, quarter, index, dst=None):
        copy = remote(
            src, halo.at[1 - core, quarter] if dst is None else dst,
            fwd_send.at[index], halo_recv.at[1], in_pair(step),
        )

        @pl.when(paired)
        def _():
            copy.start()

        pair_copies.append(copy)

    def to_pair_part(step, quarter, part, index):
        to_pair(
            step, ring.at[quarter, rows(part)], quarter, index,
            halo.at[1 - core, quarter, rows(part)],
        )

    for part in range(PARTS):
        ring_send(2, c, part, part, ring.at[c, rows(part)])
        ring_send(-2, c, PARTS - 1 - part, 2 * PARTS - 1 - part, ring.at[c, rows(PARTS - 1 - part)])
    to_pair(1, ring.at[c], c, 4)
    to_pair(-1, ring.at[c], c, 5)
    to_sibling(ring.at[c], c, 0)

    def near_shards():
        below, above = quarters[-1], quarters[1]
        for part in range(PARTS):
            last = PARTS - 1 - part
            ring_wait(below, part, part)
            if part < PARTS // 2:
                ring_send(2, below, part, 2 * PARTS + part)
            ring_wait(above, last, PARTS + last)
            if part < PARTS // 2:
                ring_send(-2, above, last, 2 * PARTS + last)
            to_pair_part(1, below, part, 6 + part)
            to_pair_part(-1, above, last, 6 + PARTS + last)
        to_sibling(ring.at[below], below, 1)
        to_sibling(ring.at[above], above, 2)

    def far_shard():
        for part in range(PARTS):
            ring_wait(quarters[2], part, 2 * PARTS + part)
        to_sibling(ring.at[quarters[2]], quarters[2], 3)

    def spread_news(k):
        for offset in NEXT:
            pl.semaphore_signal(
                news.at[k], inc=1, device_id=(2 * chip_at(offset) + core, c),
                device_id_type=pl.DeviceIdType.MESH,
            )

    def hear_news(k):
        pl.semaphore_wait(news.at[k], len(NEXT))

    spread_news(0)

    lane = lax.broadcasted_iota(jnp.int32, (128, 384), 1)
    column_of = lax.broadcasted_iota(jnp.int32, (128, 384), 0)
    first = 2 * (lane & 63) + (lane >> 7) - 1
    pairs = jnp.where(
        jnp.logical_or(column_of == first, column_of == first + 1), 1.0, 0.0
    ).astype(BF)
    low = lax.broadcasted_iota(jnp.int32, (64, 128), 1) < 64

    loads[1].wait()
    for f in range(2):
        pool[0, pl.ds(f * 1024, 1024), :] = dot(
            s_v[f].reshape(1024, 128), pairs[:, 128:256]
        )
        height = [pool[0, pl.ds(f * 1024 + h, 64, stride=16), :] for h in range(16)]
        for j in range(4):
            upper = height[4 * j] + height[4 * j + 1]
            lower = height[4 * j + 2] + height[4 * j + 3]
            sq_v[pl.ds(64 * f, 64), 128 * j : 128 * j + 128] = jnp.where(low, upper, lower).astype(BF)

    loads[2].wait()
    for f in range(2):
        sums = dot(x_v[f].reshape(1024, 128), pairs)
        for b in range(3):
            pool[1 + b, pl.ds(f * 1024, 1024), :] = sums[:, 128 * b : 128 * b + 128]
    hear_news(0)
    spread_news(1)
    near_shards()
    hear_news(1)
    spread_news(2)
    for f in range(2):
        for b in range(3):
            height = [pool[1 + b, pl.ds(f * 1024 + h, 64, stride=16), :] for h in range(16)]
            total = (
                [height[0]] + [height[h] + height[h + 1] for h in range(15)] + [height[15]]
            )
            for a in range(3):
                for j in range(4):
                    q_v[f, pl.ds((3 * a + b) * 64, 64), 128 * j : 128 * j + 128] = jnp.where(
                        low, total[4 * j + a], total[4 * j + a + 2]
                    ).astype(BF)
    loads[3].wait()
    hear_news(2)
    spread_news(3)
    far_shard()

    own = ring[...].reshape(256, 512)
    taps = dot(tw_v[...].reshape(768, 256), own)
    a_v[0] = taps[0:256] + taps[256:512]
    a_v[1] = taps[256:512] + taps[512:768]
    t_own = dot_nt(sq_v[...], own)

    dst = halo.at[1 - core]
    pltpu.make_async_copy(dst, dst, halo_recv.at[0]).wait()

    @pl.when(paired)
    def _():
        dst = halo.at[core]
        pltpu.make_async_copy(dst, dst, halo_recv.at[1]).wait()

    @pl.when(jnp.logical_not(paired))
    def _():
        halo[core] = jnp.zeros((4, 64, 512), BF)

    before = halo[0].reshape(256, 512)
    after = halo[1].reshape(256, 512)
    g_v[0] = ((a_v[0] + dot(tw_v[2], before)) * 0.125).astype(BF)
    g_v[1] = ((a_v[1] + dot(tw_v[0], after)) * 0.125).astype(BF)

    def put(dst, at, value):
        count = value.shape[0] // 16
        for side in range(2):
            piece = value[:, 128 * side : 128 * side + 128].reshape(count, 16, 128)
            dst[at : at + count, side] = piece.astype(dst.dtype)

    def spatial(dst, at, first_tap, last_tap):
        taps = slice(64 * first_tap, 64 * last_tap)
        put(dst, at, dot_nt(q_v[0, taps], g_v[0]) + dot_nt(q_v[1, taps], g_v[1]))

    def lower_half(dst):
        t_after = dot_nt(sq_v[64:128], after)
        t_before = dot_nt(sq_v[0:64], before)
        put(dst, 0, (t_own[0:64] + t_after) * 0.125)
        put(dst, 4, (t_own[0:64] + t_own[64:128]) * 0.125)
        put(dst, 8, (t_own[64:128] + t_before) * 0.125)
        spatial(dst, 12, 0, 3)

    def upper_half(dst):
        spatial(dst, 0, 3, 9)

    exchange = remote(given, xch, xch_send, xch_recv, sibling)

    @pl.when(core == 0)
    def _():
        upper_half(given)
        exchange.start()
        lower_half(kept)

    @pl.when(core == 1)
    def _():
        lower_half(given)
        exchange.start()
        upper_half(kept)

    def input_products(f):
        p_v[...] = dot(sw_v[...].reshape(576, 256), g_v[f]).reshape(9, 64, 512)

    cell = lax.broadcasted_iota(jnp.int32, (16, 512), 1)

    def input_parities(f):
        def tile(i, carry):
            here = pl.ds(pl.multiple_of(16 * i, 16), 16)
            tops, bottoms = [], []
            for b in range(3):
                t0, t1, t2 = p_v[b, here, :], p_v[3 + b, here, :], p_v[6 + b, here, :]
                tops.append(t0 + t1 + jnp.where(cell >= 64, pltpu.roll(t2, 64, 1), 0.0))
                bottoms.append(t1 + t2 + jnp.where(cell < 448, pltpu.roll(t0, 448, 1), 0.0))
            for r, (u0, u1, u2) in enumerate((tops, bottoms)):
                even = u0 + u1 + jnp.where((cell & 63) != 0, pltpu.roll(u2, 1, 1), 0.0)
                odd = u1 + u2 + jnp.where((cell & 63) != 63, pltpu.roll(u0, 511, 1), 0.0)
                for j in range(4):
                    cut = slice(128 * j, 128 * j + 128)
                    xe_v[r, j, here, 0:128] = even[:, cut].astype(BF)
                    xe_v[r, j, here, 128:256] = odd[:, cut].astype(BF)
            return carry

        lax.fori_loop(0, 4, tile, 0)

    k_of = lax.broadcasted_iota(jnp.int32, (256, 256), 0)
    w_of = lax.broadcasted_iota(jnp.int32, (256, 256), 1)
    place = ((k_of >> 6) & 1) * 128 + 2 * (k_of & 63) + (k_of >> 7)
    weave = jnp.where(w_of == place, 1.0, 0.0).astype(BF)

    def input_output(f):
        woven = dot(xe_v[...].reshape(512, 256), weave).reshape(2, 4, 64, 256)
        for r in range(2):
            for j in range(4):
                for k in range(2):
                    h = 2 * (2 * j + k) + r
                    z_v[pl.ds(h, 64, stride=16), :] = woven[r, j, :, 128 * k : 128 * k + 128]
        ig_v[f] = z_v[0:1024].reshape(64, 16, 128).astype(BF)

    exchange.wait_recv()
    half_v[...] = (kept[...] + xch[...].astype(F32)).astype(BF).reshape(PIECES, 16, 128)
    hear_news(3)

    large = lax.rem(x + y + zl + core, 2) == 0
    large_at, small_at = 2 * column, 32 + column

    for slot, offset in enumerate(FAR_FIRST):
        owner = chip_at(offset)
        owner_column = lax.div(owner, 2)
        owner_large = large if sum(offset) % 2 == 0 else jnp.logical_not(large)

        @pl.when(owner_large)
        def _():
            remote(
                half_v.at[pl.ds(2 * owner_column, 2)], rs_v.at[pl.ds(2 * slot, 2)],
                rs_send, rs_recv, (2 * owner + core, c),
            ).start()

        @pl.when(jnp.logical_not(owner_large))
        def _():
            remote(
                half_v.at[pl.ds(32 + owner_column, 1)], rs_v.at[pl.ds(slot, 1)],
                rs_send, rs_recv, (2 * owner + core, c),
            ).start()

    loads[4].wait()
    input_products(0)
    input_parities(0)
    input_output(0)

    def own_piece(at, count):
        dst = rs_v.at[pl.ds(0, count * (CHIPS - 1))]
        pltpu.make_async_copy(dst, dst, rs_recv).wait()
        total = half_v[pl.ds(at, count)].astype(F32)
        for slot in range(CHIPS - 1):
            total = total + rs_v[count * slot : count * slot + count].astype(F32)
        here = pl.ds(core * PIECES + at, count)
        gr_v[here] = total.astype(BF)
        src = gr_v.at[here]

        def hand_out(target):
            for side in (1, 0):
                remote(src, src, ag_send.at[side], ag_recv.at[core], (2 * target + side, c)).start()

        remote(src, src, ag_send.at[1 - core], ag_recv.at[core], sibling).start()

        for i, j, k in [(0, 0, 0)] + FAR_FIRST[::-1]:
            target = 8 * i + 2 * j + k

            @pl.when(target != chip)
            def _():
                hand_out(target)


    @pl.when(large)
    def _():
        own_piece(large_at, 2)

    @pl.when(jnp.logical_not(large))
    def _():
        own_piece(small_at, 1)

    input_products(1)
    input_parities(1)
    input_output(1)

    def rest(count, sem):
        dst = gr_v.at[pl.ds(0, count)]
        pltpu.make_async_copy(dst, dst, sem).wait()

    @pl.when(large)
    def _():
        rest(PIECES - 2, ag_recv.at[core])

    @pl.when(jnp.logical_not(large))
    def _():
        rest(PIECES - 1, ag_recv.at[core])


    rest(PIECES, ag_recv.at[1 - core])

    for copy in sent:
        copy.wait_send()

    @pl.when(paired)
    def _():
        for copy in pair_copies:
            copy.wait_send()

    exchange.wait_send()

    @pl.when(large)
    def _():
        rest(PIECES - 2, rs_send)
        rest(2 * (CHIPS - 1), ag_send.at[core])
        rest(2 * CHIPS, ag_send.at[1 - core])

    @pl.when(jnp.logical_not(large))
    def _():
        rest(PIECES - 1, rs_send)
        rest(CHIPS - 1, ag_send.at[core])
        rest(CHIPS, ag_send.at[1 - core])


def finish(ig_v, gr_v, ig_out, sp_out, te_out, wide_v, sem):
    scale = 1.0 / math.sqrt(128 * 16 * 128)
    stores = [pltpu.make_async_copy(ig_v, ig_out, sem.at[8])]
    stores[0].start()
    for k in range(8):
        pieces = gr_v[12 * k : 12 * k + 12].reshape(6, 2, 16, 128)
        for side in range(2):
            wide_v[6 * k : 6 * k + 6, :, 128 * side : 128 * side + 128] = (
                pieces[:, side].astype(F32) * scale
            )
        dst = te_out.at[pl.ds(6 * k, 6)] if k < 2 else sp_out.at[pl.ds(6 * k - 12, 6)]
        store = pltpu.make_async_copy(wide_v.at[pl.ds(6 * k, 6)], dst, sem.at[k])
        store.start()
        stores.append(store)
    for store in stores:
        store.wait()


def shards(inputs, saved, cotangent, spatial_w, temporal_w):
    vmem = pltpu.VMEM
    dma = pltpu.SemaphoreType.DMA
    input_grad, grads = pl.pallas_call(
        kernel,
        out_shape=(
            pltpu.VMEM((2, 64, 16, 128), BF),
            pltpu.VMEM((2 * PIECES, 16, 128), BF),
        ),
        in_specs=[pl.BlockSpec(memory_space=pl.ANY)] * 5,
        out_specs=(
            pl.BlockSpec(memory_space=pltpu.VMEM),
            pl.BlockSpec(memory_space=pltpu.VMEM),
        ),
        scratch_shapes=[
            vmem((2, 64, 16, 128), BF),
            vmem((2, 64, 16, 128), BF),
            vmem((3, 3, 64, 256), BF),
            vmem((3, 256, 256), BF),
            vmem((4, 64, 512), BF),
            vmem((2, 4, 64, 512), BF),
            vmem((4, 2048 + 16, 128), F32),
            vmem((2, 576, 512), BF),
            vmem((128, 512), BF),
            vmem((2, 256, 512), F32),
            vmem((2, 256, 512), BF),
            vmem((9, 64, 512), F32),
            vmem((2, 4, 64, 256), BF),
            vmem((1024 + 16, 128), F32),
            vmem((24, 2, 16, 128), BF),
            vmem((24, 2, 16, 128), F32),
            vmem((24, 2, 16, 128), BF),
            vmem((PIECES, 16, 128), BF),
            vmem((2 * (CHIPS - 1), 16, 128), BF),
            dma((5,)),
            dma((3 * PARTS,)),
            dma((3 * PARTS,)),
            dma((6 + 2 * PARTS,)),
            dma((2,)),
            dma, dma,
            dma, dma,
            dma((2,)), dma((2,)),
            pltpu.SemaphoreType.REGULAR((ROUNDS,)),
        ],
        compiler_params=pltpu.CompilerParams(
            collective_id=0, has_side_effects=True, vmem_limit_bytes=56 * 1024 * 1024
        ),
        name="space_time_backward",
    )(inputs, saved, cotangent, spatial_w, temporal_w)
    input_grad = pltpu.with_memory_space_constraint(input_grad, pltpu.VMEM)
    grads = pltpu.with_memory_space_constraint(grads, pltpu.VMEM)
    input_grad, spatial, temporal = pl.pallas_call(
        finish,
        out_shape=(
            jax.ShapeDtypeStruct((2, 64, 16, 128), BF),
            jax.ShapeDtypeStruct((36, 16, 256), F32),
            jax.ShapeDtypeStruct((12, 16, 256), F32),
        ),
        in_specs=[pl.BlockSpec(memory_space=pltpu.VMEM)] * 2,
        out_specs=[pl.BlockSpec(memory_space=pl.ANY)] * 3,
        scratch_shapes=[
            vmem((48, 16, 256), F32),
            dma((9,)),
        ],
        name="scale_gradients",
    )(input_grad, grads)
    return (input_grad, spatial.reshape(3, 3, 64, 256), temporal.reshape(3, 64, 256))


def solution(mesh):
    return jax.shard_map(
        shards,
        mesh=mesh,
        in_specs=(
            P("frames", "chan", None, None),
            P("frames", "chan", None, None),
            P("frames", "chan", None),
            P(None, None, "chan", None),
            P(),
        ),
        out_specs=(
            P("frames", "chan", None, None),
            P(None, None, "chan", None),
            P(None, "chan", None),
        ),
        check_vma=False,
    )
```
